32 devices in a mesh: seq: 16 (over z, y, core), dp: 2 (over x).
Axes of the slice: x: 2, y: 2, z: 4, core: 2. Of those that a mesh axis runs over, the one named last changes fastest.
Arguments:
- genome: bfloat16 [2, 32768, 512], P('dp', 'seq'), may hold values from -6 to 6
- conv_weight: bfloat16 [3, 512, 512], replicated, may hold values from -0.15625 to 0.15625
- upstream: bfloat16 [2, 32768, 512], P('dp', 'seq'), may hold values from -6 to 6
Outputs:
- output: bfloat16 [2, 32768, 512], P('dp', 'seq')
- grad_genome: bfloat16 [2, 32768, 512], P('dp', 'seq')
- grad_weight: float32 [3, 512, 512], replicated
The draws below stay inside these ranges and needn't reach their ends.
All inputs are finite; a program needn't handle non-finite values.
Results may differ from the reference program's by a relative error of at most 0.0035.
Values may be sent and summed in bfloat16 or wider, within the bound.
No kernel may reach another device: no remote copies, remote signals or barrier semaphores. Data moves between devices by JAX's collectives and lax.ppermute only.
A program may use at most 128 MiB of HBM per device.

```python
import jax
import jax.numpy as jnp
from jax import lax

C = 512
DILATION_BINS = 4096
BINS = 32768
GENOMES = 2


def block_scale(own_key, dims, split, least, high):
    loudness = 1.0
    for position, parts in split:
        draws = jax.random.uniform(jax.random.fold_in(jax.random.fold_in(own_key, 6), position), (parts,), jnp.float32, least / len(split), high / len(split))
        loudness = loudness * jnp.repeat(jnp.exp(draws), dims[position] // parts).reshape((-1,) + (1,) * (len(dims) - 1 - position))
    return loudness


def scatter_about(rng, extent, width, reach, shards=(), kind=jnp.bfloat16):
    loudness = block_scale(rng, extent, shards, -0.22, 0.18) if shards else 1.0
    array = jax.random.normal(rng, extent, jnp.float32) * width * loudness
    return jnp.minimum(jnp.maximum(array, -reach), reach).astype(kind)


def setup_inputs(seed: int = 0) -> dict:
    keys = jax.random.split(jax.random.key(seed), 4)
    genome = scatter_about(keys[0], (GENOMES, BINS, C), 1.0, 6.0, ((0, 2), (1, 16)))
    conv_weight = scatter_about(keys[1], (3, C, C), (3 * C) ** -0.5, 0.15625)
    upstream = scatter_about(keys[2], (GENOMES, BINS, C), 1.0, 6.0, ((0, 2), (1, 16)))
    return dict(genome=genome, conv_weight=conv_weight, upstream=upstream)


def taps(receptive_field):
    padded_input = jnp.pad(receptive_field, ((0, 0), (DILATION_BINS, DILATION_BINS), (0, 0)))
    return (padded_input[:, :-2 * DILATION_BINS], padded_input[:, 2 * DILATION_BINS:])

def mixing(left, right):
    return jnp.einsum('gbc,cd->gbd', left, right, precision=lax.Precision.HIGHEST)

def outer_sum(left, right):
    return jnp.einsum('gbc,gbd->cd', left, right, precision=lax.Precision.HIGHEST)

def reference(genome, conv_weight, upstream):
    inputs = genome.astype(jnp.float32)
    act_full, slope_fn = jax.vjp(jax.nn.gelu, inputs)
    act = act_full.astype(jnp.bfloat16).astype(jnp.float32)
    act_prev, act_next = taps(act)
    weights = conv_weight.astype(jnp.float32)
    conv = mixing(act_prev, weights[0]) + mixing(act, weights[1]) + mixing(act_next, weights[2])
    output = (inputs + conv).astype(jnp.bfloat16)
    grads = upstream.astype(jnp.float32)
    up_prev, up_next = taps(grads)
    grad_act = mixing(up_next, weights[0].T) + mixing(grads, weights[1].T) + mixing(up_prev, weights[2].T)
    grad_genome = (grads + slope_fn(grad_act)[0]).astype(jnp.bfloat16)
    grad_weight = jnp.stack([outer_sum(act_prev, grads), outer_sum(act, grads), outer_sum(act_next, grads)])
    return (output, grad_genome, grad_weight)
```

```python
import jax
import jax.numpy as jnp
from jax import lax
from jax.sharding import PartitionSpec as P

DILATION_BINS = 4096
BF16, F32 = jnp.bfloat16, jnp.float32


def rows_of(value, start, size, dim=0):
    return lax.dynamic_slice_in_dim(value, start, size, dim)


def mixing(left, right):
    return jnp.einsum("bc,cd->bd", left, right, preferred_element_type=F32)


def mixing_back(left, right):
    return jnp.einsum("bd,cd->bc", left, right, preferred_element_type=F32)


def outer_sum(left, right):
    return jnp.einsum("bc,bd->cd", left, right, preferred_element_type=F32)


class Group:
    def __init__(self, axis, position, count, pairs_of_shift):
        self.axis, self.position, self.count, self.pairs = axis, position, count, pairs_of_shift

    def scatter_sum(self, value):
        size = value.shape[1] // self.count
        total = rows_of(value, self.position * size, size, 1)
        for shift in range(1, self.count):
            there = lax.rem(self.position + shift, self.count)
            total = total + lax.ppermute(rows_of(value, there * size, size, 1), self.axis, self.pairs(shift))
        return total

    def gather(self, value):
        size = value.shape[1]
        whole = jnp.zeros((value.shape[0], size * self.count, value.shape[2]), value.dtype)
        whole = lax.dynamic_update_slice_in_dim(whole, value, self.position * size, 1)
        for shift in range(1, self.count):
            source = lax.rem(self.position + self.count - shift, self.count)
            part = lax.ppermute(value, self.axis, self.pairs(shift))
            whole = lax.dynamic_update_slice_in_dim(whole, part, source * size, 1)
        return whole


def per_device(genome, conv_weight, upstream):
    genome, upstream = genome[0], upstream[0]
    bins, chans = genome.shape
    half, cols = bins // 2, chans // 2
    count = lax.axis_size("seq")
    index = lax.axis_index("seq")
    tap = DILATION_BINS // bins
    side = lax.rem(index // tap, 2)
    is_even = side == 0
    own_start, oth_start = side * half, (1 - side) * half

    def even(i):
        return (i // tap) % 2 == 0

    swap_pairs = [(i, i + tap if even(i) else i - tap) for i in range(count)]
    outer_pairs = [(i, i - 2 * tap if even(i) else i + 2 * tap) for i in range(count)]
    outer_pairs = [(i, j) for i, j in outer_pairs if 0 <= j < count]
    inner_pairs = [(j, i) for i, j in outer_pairs]

    def swap(value):
        return lax.ppermute(value, "seq", swap_pairs)

    def outward(value):
        return lax.ppermute(value, "seq", outer_pairs)

    def inward(value):
        return lax.ppermute(value, "seq", inner_pairs)

    w_mid = conv_weight[1]
    w_far = jnp.where(is_even, conv_weight[0], conv_weight[2])
    w_near = jnp.where(is_even, conv_weight[2], conv_weight[0])

    step = half // 2
    u_own = rows_of(upstream, own_start, half)
    u_parts = [swap(rows_of(upstream, oth_start + k * step, step)) for k in range(2)]
    x_parts = [swap(rows_of(genome, oth_start, half)[:, k * cols : (k + 1) * cols]) for k in range(2)]
    x_own = rows_of(genome, own_start, half)
    u_oth_far = outward(u_own)
    act, slope_own = jax.vjp(jax.nn.gelu, x_own.astype(F32))
    a_own = act.astype(BF16)
    a_oth_far = outward(a_own)
    u_own_far = jnp.concatenate([inward(part) for part in u_parts], 0)
    u_oth = jnp.concatenate(u_parts, 0)

    dp_index, dp_count = lax.axis_index("dp"), lax.axis_size("dp")
    core = Group("seq", lax.rem(index, tap), tap, lambda s: [(i, i - i % tap + (i % tap + s) % tap) for i in range(count)])
    other = Group("dp", dp_index, dp_count, lambda s: [(i, (i + s) % dp_count) for i in range(dp_count)])
    span = 2 * tap
    along = Group("seq", index // span, count // span, lambda s: [(i, (i + s * span) % count) for i in range(count)])

    own_act = jax.nn.gelu(genome.astype(F32)).astype(BF16)
    mid = outer_sum(own_act, upstream).reshape(2, cols, chans)
    mid = other.scatter_sum(core.scatter_sum(mid))

    def outer_parts(k):
        a_k = a_own[:, k * cols : (k + 1) * cols]
        x_k, slope = jax.vjp(jax.nn.gelu, x_parts[k].astype(F32))
        b_k = x_k.astype(BF16)
        far = outer_sum(a_k, u_oth) + outer_sum(b_k, u_oth_far)
        near = outer_sum(b_k, u_own) + outer_sum(a_k, u_own_far)
        return b_k, slope, jnp.stack([far, near])

    def finish(parts, taps):
        total = along.scatter_sum(parts)
        side_sum = total[-2:]
        side_sum = jnp.where(is_even, side_sum, side_sum[::-1])
        total = jnp.concatenate([total[:-2], side_sum], 0)
        total = total + swap(total)
        return core.gather(other.gather(along.gather(total.astype(BF16))))

    a_parts, gg_back, sums = [], [], []
    for k in range(2):
        b_k, slope, outer = outer_parts(k)
        a_parts.append(b_k)
        span_k = slice(k * cols, (k + 1) * cols)
        grad_act = (
            mixing_back(u_own, w_near[span_k])
            + mixing_back(u_oth, w_mid[span_k])
            + mixing_back(u_oth_far, w_far[span_k])
        )
        gg = (u_oth[:, span_k].astype(F32) + slope(grad_act)[0]).astype(BF16)
        gg_back.append(swap(gg))
        outer = other.scatter_sum(core.scatter_sum(outer))
        sums.append(finish(jnp.concatenate([mid, outer], 0) if k == 0 else outer, None))
    a_own_far = jnp.concatenate([inward(part) for part in a_parts], 1)
    a_oth = jnp.concatenate(a_parts, 1)
    x_oth = jnp.concatenate(x_parts, 1)

    out_back = []
    for k in range(2):
        r = slice(k * step, (k + 1) * step)
        conv = mixing(a_own[r], w_far) + mixing(a_oth[r], w_mid) + mixing(a_oth_far[r], w_near)
        out_back.append(swap((x_oth[r].astype(F32) + conv).astype(BF16)))

    grad_act = mixing_back(u_oth, w_far) + mixing_back(u_own, w_mid) + mixing_back(u_own_far, w_near)
    gg_own = (u_own.astype(F32) + slope_own(grad_act)[0]).astype(BF16)
    conv = mixing(a_oth, w_near) + mixing(a_own, w_mid) + mixing(a_own_far, w_far)
    out_own = (x_own.astype(F32) + conv).astype(BF16)

    def placed(own, back):
        return jnp.where(is_even, jnp.concatenate([own, back], 0), jnp.concatenate([back, own], 0))[None]

    output = placed(out_own, jnp.concatenate(out_back, 0))
    grad_genome = placed(gg_own, jnp.concatenate(gg_back, 1))
    first, second = sums
    grad_weight = jnp.stack(
        [
            jnp.concatenate([first[2], second[0]], 0),
            jnp.concatenate([first[0], first[1]], 0),
            jnp.concatenate([first[3], second[1]], 0),
        ]
    ).astype(F32)
    return (output, grad_genome, grad_weight)


def solution(mesh):
    return jax.shard_map(
        per_device,
        mesh=mesh,
        in_specs=(P("dp", "seq", None), P(), P("dp", "seq", None)),
        out_specs=(P("dp", "seq", None), P("dp", "seq", None), P()),
        check_vma=False,
    )
```

```python
import functools

import jax
import jax.numpy as jnp
from jax import lax
from jax.experimental import pallas as pl
from jax.experimental.pallas import tpu as pltpu
from jax.sharding import PartitionSpec as P

DILATION_BINS = 4096
BF16, F32 = jnp.bfloat16, jnp.float32
VMEM_BYTES = 40 * 1024 * 1024
SIDE, CORE, DP, ALONG = range(4)
HBM = pl.BlockSpec(memory_space=pltpu.HBM)
WHOLE = pl.BlockSpec(memory_space=pltpu.VMEM)


def shape_of(shape, dtype):
    return jax.ShapeDtypeStruct(shape, dtype)


TOKEN = jax.ShapeDtypeStruct((8, 128), F32)


class Device:
    def __init__(self, meta):
        self.meta, self.token = meta, None


def call(
    body, device, operands, in_specs, outs, out_specs, grid=(), scratch=(), aliases=None, name=None, after=()
):
    first = device.token is None
    n_in, single = len(operands), not isinstance(outs, list)
    outs, out_specs = ([outs], [out_specs]) if single else (outs, out_specs)
    n_out = len(outs)
    tokens = [*after] if first else [device.token, *after]

    def chained(meta, *refs):
        rest = refs[n_in + len(tokens) :]
        body(meta, *refs[:n_in], *rest[:n_out], *rest[n_out + 1 :])

    results = pl.pallas_call(
        chained,
        grid_spec=pltpu.PrefetchScalarGridSpec(
            num_scalar_prefetch=1, grid=grid, in_specs=[*in_specs, *[HBM] * len(tokens)], out_specs=[*out_specs, HBM],
            scratch_shapes=list(scratch),
        ),
        out_shape=[*outs, TOKEN],
        input_output_aliases=aliases or {},
        compiler_params=pltpu.CompilerParams(vmem_limit_bytes=VMEM_BYTES),
        cost_estimate=pl.CostEstimate(flops=1, bytes_accessed=200_000, transcendentals=0),
        name=name,
    )(device.meta, *operands, *tokens)
    device.token = results[-1]
    return results[0] if single else results[:-1]


def gelu_parts(x):
    k = 0.7978845608028654
    square = x * x
    t = jnp.tanh(k * (x * (1.0 + 0.044715 * square)))
    return t, square, k


def gelu(x):
    t, _, _ = gelu_parts(x)
    return x * (0.5 * (1.0 + t))


def gelu_and_slope(x):
    t, square, k = gelu_parts(x)
    cdf = 0.5 * (1.0 + t)
    slope = cdf + 0.5 * x * (1.0 - t * t) * (k + (3 * 0.044715 * k) * square)
    return x * cdf, slope


def mm(left, right):
    return lax.dot_general(left, right, (((1,), (0,)), ((), ())), preferred_element_type=F32)


def mm_back(left, right):
    return lax.dot_general(left, right, (((1,), (1,)), ((), ())), preferred_element_type=F32)


def mm_outer(left, right):
    return lax.dot_general(left, right, (((0,), (0,)), ((), ())), preferred_element_type=F32)


def cut_body(plan, n_in, meta, *refs):
    ins, outs, sems = refs[:n_in], refs[n_in:-1], refs[-1]
    copies = []
    for n, (which, own, col, rows, cols) in enumerate(plan):
        start = (meta[SIDE] if own else 1 - meta[SIDE]) * rows
        window = ins[which].at[pl.ds(pl.multiple_of(start, rows), rows), pl.ds(col, cols)]
        copies.append(pltpu.make_async_copy(window, outs[n], sems.at[n]))
    for copy in copies:
        copy.start()
    for copy in copies:
        copy.wait()


def cut(device, operands, plan, name):
    outs = [shape_of((rows, cols), BF16) for _, _, _, rows, cols in plan]
    return call(
        functools.partial(cut_body, plan, len(operands)), device, operands, [HBM] * len(operands), outs,
        [HBM] * len(plan), scratch=[pltpu.SemaphoreType.DMA((len(plan),))], name=name,
    )


def split_into(total, position, count, keep, sends):
    size = total.shape[1] // count
    for shift, ref in enumerate((keep, *sends)):
        there = lax.rem(position + shift, count)
        ref[...] = total[:, pl.ds(pl.multiple_of(there * size, size), size), :]


def mid_body(steps, count, meta, x, u, *refs):
    *slices, total = refs
    i = pl.program_id(0)

    @pl.when(i == 0)
    def _():
        total[...] = jnp.zeros_like(total)

    cols = total.shape[2]
    product = mm_outer(gelu(x[...].astype(F32)).astype(BF16), u[...])
    for part in range(2):
        total[part] += product[:, part * cols : (part + 1) * cols]
    send_slices(i == steps - 1, count, meta, total, slices)


def send_slices(last, count, meta, total, slices):
    @pl.when(last)
    def _():
        for part in range(2):
            split_into(total.at[part : part + 1], meta[CORE], count, slices[part], [slices[2 + part]])


def reduce_body(sizes, n_out, place, swap_sides, meta, *refs):
    n_in = sum(sizes)
    ins, outs, total = refs[:n_in], refs[n_in:-1], refs[-1]
    first = lead = 0
    for size in sizes:
        value = ins[first][...]
        for ref in ins[first + 1 : first + size]:
            value = value + ref[...]
        first += size
        parts = value.shape[0]
        if not swap_sides:
            total[lead : lead + parts] = value
        else:
            plain = parts - 2
            if plain:
                total[lead : lead + plain] = value[:plain]
            for part in range(2):
                total[lead + plain + part] = jnp.where(meta[SIDE] == 0, value[plain + part], value[plain + 1 - part])
        lead += parts
    if n_out > 1:
        split_into(total, meta[place], n_out, outs[0], outs[1:])
    else:
        outs[0][...] = total[...].astype(outs[0].dtype)


def reduce(device, groups, n_out=1, place=None, swap_sides=False, dtype=F32, name=None, after=()):
    _, rows, cols = groups[0][0].shape
    k = sum(group[0].shape[0] for group in groups)
    values = [value for group in groups for value in group]
    outs = [shape_of((k, rows // n_out, cols), dtype)] * n_out
    body = functools.partial(reduce_body, [len(group) for group in groups], n_out, place, swap_sides)
    return call(
        body, device, values, [WHOLE] * len(values), outs, [WHOLE] * n_out,
        scratch=[pltpu.VMEM((k, rows, cols), F32)], name=name, after=after,
    )


def gather_body(count, place, meta, *refs):
    ins, out = refs[:count], refs[count]
    size = ins[0].shape[1]
    for shift, ref in enumerate(ins):
        source = lax.rem(meta[place] + count - shift, count)
        out[:, pl.ds(pl.multiple_of(source * size, size), size), :] = ref[...]


def gather(device, values, place, name=None):
    count = len(values)
    k, rows, cols = values[0].shape
    return call(
        functools.partial(gather_body, count, place), device, values, [WHOLE] * count,
        shape_of((k, rows * count, cols), BF16), WHOLE, name=name,
    )


def write_taps_body(count, targets, meta, *refs):
    ins = refs[:count]
    out, wide, sems = refs[count:]
    size = ins[0].shape[1]
    for shift, ref in enumerate(ins):
        source = lax.rem(meta[CORE] + count - shift, count)
        wide[:, pl.ds(pl.multiple_of(source * size, size), size), :] = ref[...].astype(F32)
    copies = []
    for n, (tap, col) in enumerate(targets):
        window = out.at[tap, :, pl.ds(col, wide.shape[2])]
        copies.append(pltpu.make_async_copy(wide.at[n], window, sems.at[n]))
    for copy in copies:
        copy.start()
    for copy in copies:
        copy.wait()


def write_taps(device, values, targets, shape, name):
    count = len(values)
    k, rows, cols = values[0].shape
    return call(
        functools.partial(write_taps_body, count, targets), device, values, [WHOLE] * count,
        shape_of(shape, F32), HBM, scratch=[pltpu.VMEM((k, rows * count, cols), F32), pltpu.SemaphoreType.DMA((k,))],
        name=name,
    )


def act_body(meta, x, *acts):
    act = gelu(x[...].astype(F32)).astype(BF16)
    cols = acts[0].shape[1]
    for n, ref in enumerate(acts):
        ref[...] = act[:, n * cols : (n + 1) * cols]


def mm_parts(lefts, weight):
    cols = lefts[0].shape[1]
    return sum(mm(left[...], weight[0, n * cols : (n + 1) * cols]) for n, left in enumerate(lefts))


def oth_out_body(meta, x0, x1, oth0, oth1, far0, far1, own0, own1, w_near, w_mid, w_far, out):
    cols = x0.shape[1]
    conv = mm_parts((oth0, oth1), w_mid) + mm_parts((far0, far1), w_near) + mm_parts((own0, own1), w_far)
    out[:, :cols] = (x0[...].astype(F32) + conv[:, :cols]).astype(BF16)
    out[:, cols:] = (x1[...].astype(F32) + conv[:, cols:]).astype(BF16)


def own_out_body(meta, x, own0, own1, oth0, oth1, far0, far1, w_near, w_mid, w_far, out):
    conv = mm_parts((own0, own1), w_mid) + mm_parts((oth0, oth1), w_near) + mm_parts((far0, far1), w_far)
    out[...] = (x[...].astype(F32) + conv).astype(BF16)


def outer_body(steps, count, meta, own0, own1, oth0, oth1, far0, far1, u_own, u_oth, u_far, *refs):
    *slices, total = refs
    i = pl.program_id(0)

    @pl.when(i == 0)
    def _():
        total[...] = jnp.zeros_like(total)

    cols = own0.shape[1]
    for n, (own, oth, far) in enumerate(((own0, oth0, far0), (own1, oth1, far1))):
        rows = slice(n * cols, (n + 1) * cols)
        total[0, rows] += mm_outer(own[...], u_oth[...]) + mm_outer(oth[...], u_far[...])
        total[1, rows] += mm_outer(far[...], u_oth[...]) + mm_outer(oth[...], u_own[...])
    send_slices(i == steps - 1, count, meta, total, slices)


def mm_back_parts(lefts, weight):
    cols = lefts[0].shape[1]
    return sum(mm_back(left[...], weight[0, :, n * cols : (n + 1) * cols]) for n, left in enumerate(lefts))


def oth_grad_body(meta, x0, x1, u_own, oth0, oth1, far0, far1, w_near, w_mid, w_far, grad0, grad1):
    cols = oth0.shape[1]
    grad_act = mm_back(u_own[...], w_near[0]) + mm_back_parts((oth0, oth1), w_mid) + mm_back_parts((far0, far1), w_far)
    for n, (x, u, grad) in enumerate(((x0, oth0, grad0), (x1, oth1, grad1))):
        _, slope = gelu_and_slope(x[...].astype(F32))
        grad[...] = (u[...].astype(F32) + slope * grad_act[:, n * cols : (n + 1) * cols]).astype(BF16)


def own_grad_body(meta, x, u_own, oth0, oth1, far0, far1, w_near, w_mid, w_far, grad):
    _, slope = gelu_and_slope(x[...].astype(F32))
    u = u_own[...]
    grad_act = mm_back(u, w_mid[0]) + mm_back_parts((oth0, oth1), w_far) + mm_back_parts((far0, far1), w_near)
    grad[...] = (u.astype(F32) + slope * grad_act).astype(BF16)


def place_body(row, col, meta, part, buffer, out, sem):
    rows, cols = part.shape
    start = pl.multiple_of((1 - meta[SIDE]) * (buffer.shape[0] // 2), rows) + row
    copy = pltpu.make_async_copy(part, out.at[pl.ds(pl.multiple_of(start, 16), rows), pl.ds(col, cols)], sem)
    copy.start()
    copy.wait()


def place(device, part, buffer, row, col, name):
    return call(
        functools.partial(place_body, row, col), device, (part, buffer), [HBM, HBM],
        shape_of(buffer.shape, buffer.dtype), HBM, scratch=[pltpu.SemaphoreType.DMA], aliases={2: 0}, name=name,
    )


def per_device(genome, conv_weight, upstream):
    genome, upstream = genome[0], upstream[0]
    bins, chans = genome.shape
    half, cols = bins // 2, chans // 2
    block = half // 4
    steps = half // block
    count = lax.axis_size("seq")
    index = lax.axis_index("seq")
    tap = DILATION_BINS // bins
    span = 2 * tap
    dp_count, along_count = lax.axis_size("dp"), count // span
    side, along = lax.rem(index // tap, 2), index // span
    if along_count % 2 == 0:
        along = along ^ side
    meta = jnp.stack(
        [side, lax.rem(index, tap), lax.axis_index("dp"), along]
    ).astype(jnp.int32)

    def is_even(i):
        return (i // tap) % 2 == 0

    swap_pairs = [(i, i + tap if is_even(i) else i - tap) for i in range(count)]
    outer_pairs = [(i, i - span if is_even(i) else i + span) for i in range(count)]
    outer_pairs = [(i, j) for i, j in outer_pairs if 0 <= j < count]
    inner_pairs = [(j, i) for i, j in outer_pairs]

    def swap(value):
        return lax.ppermute(value, "seq", swap_pairs)

    def outward(value):
        return lax.ppermute(value, "seq", outer_pairs)

    def inward(value):
        return lax.ppermute(value, "seq", inner_pairs)

    def to_core(value, shift=1):
        return lax.ppermute(value, "seq", [(i, i - i % tap + (i % tap + shift) % tap) for i in range(count)])

    def to_dp(value, shift=1):
        return lax.ppermute(value, "dp", [(i, (i + shift) % dp_count) for i in range(dp_count)])

    flip = 1 if along_count % 2 == 0 else 0

    def place_along(i):
        return (i // span) ^ (flip * ((i // tap) % 2))

    def device_at(i, side, position):
        return (position ^ (flip * side)) * span + side * tap + i % tap

    def to_along(value, shift):
        pairs = [(i, device_at(i, (i // tap) % 2, (place_along(i) + shift) % along_count)) for i in range(count)]
        return lax.ppermute(value, "seq", pairs)

    def to_side(value):
        pairs = [(i, device_at(i, 1 - (i // tap) % 2, place_along(i))) for i in range(count)]
        return lax.ppermute(value, "seq", pairs)

    rows_spec = pl.BlockSpec((block, chans), lambda i, s: (i, 0))
    part_spec = pl.BlockSpec((block, cols), lambda i, s: (i, 0))
    own_spec = pl.BlockSpec((block, chans), lambda i, s: (s[SIDE] * steps + i, 0))

    w_near = pl.BlockSpec((1, chans, chans), lambda i, s: (2 - 2 * s[SIDE], 0, 0))
    w_mid = pl.BlockSpec((1, chans, chans), lambda i, s: (1, 0, 0))
    w_far = pl.BlockSpec((1, chans, chans), lambda i, s: (2 * s[SIDE], 0, 0))

    weights = (conv_weight,) * 3
    slice_specs = [pl.BlockSpec((1, chans // tap, cols), lambda i, s: (0, 0, 0))] * 4
    slices = [shape_of((1, chans // tap, cols), F32)] * 4
    total_shape = pltpu.VMEM((2, chans, cols), F32)

    device = Device(meta)

    (x_send0,) = cut(device, (genome,), [(0, False, 0, half, cols)], "cut_first")
    x_oth0 = swap(x_send0)
    a_own = call(
        act_body, device, (genome,), [own_spec], [shape_of((half, cols), BF16)] * 2, [part_spec] * 2,
        grid=(steps,), name="own_act",
    )
    a_oth_far = [outward(part) for part in a_own]
    plan = [(0, False, cols), (1, False, 0), (1, False, cols), (1, True, 0), (1, True, cols)]
    x_send1, u_send0, u_send1, u_own0, u_own1 = cut(
        device, (genome, upstream), [(which, own, col, half, cols) for which, own, col in plan], "cut_rest"
    )
    x_oth1, u_oth = swap(x_send1), [swap(u_send0), swap(u_send1)]
    u_oth_far = [outward(u_own0), outward(u_own1)]
    mid = call(
        functools.partial(mid_body, 2 * steps, tap), device, (genome, upstream), [rows_spec] * 2, slices, slice_specs,
        grid=(2 * steps,), scratch=[total_shape], name="mid_tap",
    )

    staged = (chans // tap // dp_count) % (16 * along_count) == 0

    def core_stage(parts, name, after=()):
        groups = [[keep, to_core(send)] for keep, send in zip(parts[:2], parts[2:])]
        keep, send = reduce(device, groups, dp_count, DP, name=name + "_core", after=after)
        return [keep, to_dp(send)]

    def dp_stage(groups, name, after=()):
        if not staged:
            return reduce(device, groups, name=name + "_dp", after=after)
        parts = reduce(device, groups, along_count, ALONG, name=name + "_dp", after=after)
        return [parts[0]] + [to_along(part, shift) for shift, part in enumerate(parts[1:], 1)]

    def along_stage(groups, name, after=()):
        (total,) = reduce(device, groups, swap_sides=True, name=name + "_along", after=after)
        if not staged:
            together = [[i + span * j for j in range(along_count)] for i in range(span)]
            total = lax.psum(total, "seq", axis_index_groups=together)
        return [total, to_side(total)]

    def side_stage(parts, name):
        (total,) = reduce(device, [parts], dtype=BF16, name=name + "_side")
        return [total] + [to_along(total, s) for s in range(1, along_count) if staged]

    def gather_along(parts, name):
        total = gather(device, parts, ALONG, name + "_all_along") if staged else parts[0]
        return [total] + [to_dp(total, s) for s in range(1, dp_count)]

    def gather_dp(parts, name):
        total = gather(device, parts, DP, name + "_all_dp")
        return [total] + [to_core(total, s) for s in range(1, tap)]

    def outer_taps(k, after=()):
        u_own_spec = pl.BlockSpec((block, cols), lambda i, s: (s[SIDE] * steps + i, k))
        return call(
            functools.partial(outer_body, steps, tap), device,
            (*a_own, *a_oth, *a_oth_far, upstream, u_oth[k], u_oth_far[k]),
            [*[part_spec] * 6, u_own_spec, part_spec, part_spec], slices, slice_specs,
            grid=(steps,), scratch=[total_shape], name=f"outer_taps{k}", after=after,
        )

    def oth_act(x, name, after=()):
        return call(
            act_body, device, (x,), [part_spec], shape_of((half, cols), BF16), part_spec, grid=(steps,), name=name,
            after=after,
        )

    a_oth0 = oth_act(x_oth0, "oth_act0")
    a_own_far0 = inward(a_oth0)
    mid = core_stage(mid, "mid", after=(a_oth_far[0],))
    a_oth1 = oth_act(x_oth1, "oth_act1", after=(a_oth_far[1],))
    a_own_far1 = inward(a_oth1)
    a_oth = [a_oth0, a_oth1]
    out = call(
        oth_out_body, device, (x_oth0, x_oth1, *a_oth, *a_oth_far, *a_own, *weights),
        [*[part_spec] * 8, w_near, w_mid, w_far],
        shape_of((half, chans), BF16), rows_spec, grid=(steps,), name="oth_out", after=(a_own_far0,),
    )
    out = swap(out)
    sent0 = outer_taps(0, after=(a_own_far1,))
    u_own_far0 = inward(u_oth[0])
    parts0 = core_stage(sent0, "outer0", after=(u_oth[1], u_oth_far[1], u_own_far0))
    sent1 = outer_taps(1)
    grad0, grad1 = call(
        oth_grad_body, device, (x_oth0, x_oth1, upstream, *u_oth, *u_oth_far, *weights),
        [part_spec, part_spec, own_spec, *[part_spec] * 4, w_near, w_mid, w_far],
        [shape_of((half, cols), BF16)] * 2, [part_spec] * 2, grid=(steps,), name="oth_grad",
    )
    grad0, grad1 = swap(grad0), swap(grad1)
    parts1 = core_stage(sent1, "outer1")
    u_own_far1 = inward(u_oth[1])
    parts0 = dp_stage([mid, parts0], "outer0")
    output = call(
        own_out_body, device, (genome, *a_own, *a_oth, a_own_far0, a_own_far1, *weights),
        [own_spec, *[part_spec] * 6, w_near, w_mid, w_far],
        shape_of((bins, chans), BF16), own_spec, grid=(steps,), name="own_out",
    )
    parts1 = dp_stage([parts1], "outer1")
    grad_genome = call(
        own_grad_body, device, (genome, upstream, *u_oth, u_own_far0, u_own_far1, *weights),
        [own_spec, own_spec, *[part_spec] * 4, w_near, w_mid, w_far],
        shape_of((bins, chans), BF16), own_spec, grid=(steps,), name="own_grad",
    )
    output = place(device, out, output, 0, 0, "place_out")
    parts = along_stage([parts0, parts1], "outer")
    parts = side_stage(parts, "outer")
    grad_genome = place(device, grad0, grad_genome, 0, 0, "place_grad0")
    parts = gather_along(parts, "outer")
    grad_genome = place(device, grad1, grad_genome, 0, cols, "place_grad1")
    parts = gather_dp(parts, "outer")
    targets = [(1, 0), (1, cols), (0, 0), (2, 0), (0, cols), (2, cols)]
    grad_weight = write_taps(device, parts, targets, conv_weight.shape, "write_taps")
    return (output[None], grad_genome[None], grad_weight)


def solution(mesh):
    return jax.shard_map(
        per_device,
        mesh=mesh,
        in_specs=(P("dp", "seq", None), P(), P("dp", "seq", None)),
        out_specs=(P("dp", "seq", None), P("dp", "seq", None), P()),
        check_vma=False,
    )
```

```python
import functools

import jax
import jax.numpy as jnp
from jax import lax
from jax.experimental import pallas as pl
from jax.experimental.pallas import tpu as pltpu
from jax.sharding import PartitionSpec as P

DILATION_BINS = 4096
BF16, F32 = jnp.bfloat16, jnp.float32
VMEM_BYTES = 40 * 1024 * 1024
SIDE, CORE, DP, ALONG, ALONG_BITS = range(5)
HBM = pl.BlockSpec(memory_space=pltpu.HBM)
WHOLE = pl.BlockSpec(memory_space=pltpu.VMEM)


def shape_of(shape, dtype):
    return jax.ShapeDtypeStruct(shape, dtype)


TOKEN = jax.ShapeDtypeStruct((8, 128), F32)


class Device:
    def __init__(self, meta):
        self.meta, self.token = meta, None


def call(
    body, device, operands, in_specs, outs, out_specs, grid=(), scratch=(), aliases=None, name=None, after=()
):
    first = device.token is None
    n_in, single = len(operands), not isinstance(outs, list)
    outs, out_specs = ([outs], [out_specs]) if single else (outs, out_specs)
    n_out = len(outs)
    tokens = [*after] if first else [device.token, *after]

    def chained(meta, *refs):
        rest = refs[n_in + len(tokens) :]
        body(meta, *refs[:n_in], *rest[:n_out], *rest[n_out + 1 :])

    results = pl.pallas_call(
        chained,
        grid_spec=pltpu.PrefetchScalarGridSpec(
            num_scalar_prefetch=1, grid=grid, in_specs=[*in_specs, *[HBM] * len(tokens)], out_specs=[*out_specs, HBM],
            scratch_shapes=list(scratch),
        ),
        out_shape=[*outs, TOKEN],
        input_output_aliases=aliases or {},
        compiler_params=pltpu.CompilerParams(vmem_limit_bytes=VMEM_BYTES),
        cost_estimate=pl.CostEstimate(flops=1, bytes_accessed=200_000, transcendentals=0),
        name=name,
    )(device.meta, *operands, *tokens)
    device.token = results[-1]
    return results[0] if single else results[:-1]


def gelu_parts(x):
    k = 0.7978845608028654
    square = x * x
    t = jnp.tanh(k * (x * (1.0 + 0.044715 * square)))
    return t, square, k


def gelu(x):
    t, _, _ = gelu_parts(x)
    return x * (0.5 * (1.0 + t))


def gelu_and_slope(x):
    t, square, k = gelu_parts(x)
    cdf = 0.5 * (1.0 + t)
    slope = cdf + 0.5 * x * (1.0 - t * t) * (k + (3 * 0.044715 * k) * square)
    return x * cdf, slope


def mm(left, right):
    return lax.dot_general(left, right, (((1,), (0,)), ((), ())), preferred_element_type=F32)


def mm_back(left, right):
    return lax.dot_general(left, right, (((1,), (1,)), ((), ())), preferred_element_type=F32)


def mm_outer(left, right):
    return lax.dot_general(left, right, (((0,), (0,)), ((), ())), preferred_element_type=F32)


def cut_body(plan, n_in, meta, *refs):
    ins, outs, sems = refs[:n_in], refs[n_in:-1], refs[-1]
    copies = []
    for n, (which, own, col, rows, cols) in enumerate(plan):
        start = (meta[SIDE] if own else 1 - meta[SIDE]) * rows
        window = ins[which].at[pl.ds(pl.multiple_of(start, rows), rows), pl.ds(col, cols)]
        copies.append(pltpu.make_async_copy(window, outs[n], sems.at[n]))
    for copy in copies:
        copy.start()
    for copy in copies:
        copy.wait()


def cut(device, operands, plan, name):
    outs = [shape_of((rows, cols), BF16) for _, _, _, rows, cols in plan]
    return call(
        functools.partial(cut_body, plan, len(operands)), device, operands, [HBM] * len(operands), outs,
        [HBM] * len(plan), scratch=[pltpu.SemaphoreType.DMA((len(plan),))], name=name,
    )


def split_into(total, position, count, keep, sends):
    size = total.shape[1] // count
    for shift, ref in enumerate((keep, *sends)):
        there = lax.rem(position + shift, count)
        ref[...] = total[:, pl.ds(pl.multiple_of(there * size, size), size), :].astype(ref.dtype)


def mid_body(x, u, total):
    @pl.when(pl.program_id(0) == 0)
    def _():
        total[...] = jnp.zeros_like(total)

    cols = total.shape[2]
    product = mm_outer(gelu(x[...].astype(F32)).astype(BF16), u[...])
    for part in range(2):
        total[part] += product[:, part * cols : (part + 1) * cols]


def reduce_body(sizes, n_out, place, swap_from, meta, *refs):
    ins, outs, total = refs[: sum(sizes)], refs[sum(sizes) : -1], refs[-1]
    first = lead = 0
    for size in sizes:
        value = ins[first][...].astype(F32)
        for ref in ins[first + 1 : first + size]:
            value = value + ref[...].astype(F32)
        total[lead : lead + value.shape[0]] = value
        first, lead = first + size, lead + value.shape[0]
    for part in range(swap_from, lead, 2):
        pair = total[part : part + 2]
        for n in range(2):
            total[part + n] = jnp.where(meta[SIDE] == 0, pair[n], pair[1 - n])
    if n_out > 1:
        split_into(total, meta[place], n_out, outs[0], outs[1:])
    else:
        outs[0][...] = total[...].astype(outs[0].dtype)


def reduce(device, groups, n_out=1, place=None, swap_from=None, dtype=F32, name=None, after=()):
    _, rows, cols = groups[0][0].shape
    k = sum(group[0].shape[0] for group in groups)
    values = [value for group in groups for value in group]
    dtypes = [dtype] if n_out == 1 else [F32] + [dtype] * (n_out - 1)
    outs = [shape_of((k, rows // n_out, cols), each) for each in dtypes]
    sizes = [len(group) for group in groups]
    body = functools.partial(reduce_body, sizes, n_out, place, k if swap_from is None else swap_from)
    return call(
        body, device, values, [WHOLE] * len(values), outs, [WHOLE] * n_out,
        scratch=[pltpu.VMEM((k, rows, cols), F32)], name=name, after=after,
    )


def gather_body(count, place, meta, *refs):
    ins, out = refs[:count], refs[count]
    size = ins[0].shape[1]
    for shift, ref in enumerate(ins):
        source = lax.rem(meta[place] + count - shift, count)
        out[:, pl.ds(pl.multiple_of(source * size, size), size), :] = ref[...]


def gather(device, values, place, name=None):
    count = len(values)
    k, rows, cols = values[0].shape
    return call(
        functools.partial(gather_body, count, place), device, values, [WHOLE] * count,
        shape_of((k, rows * count, cols), BF16), WHOLE, name=name,
    )


def write_taps_body(count, targets, aliased, meta, *refs):
    ins = refs[:count]
    out, wide, sems = refs[count + aliased :]
    size = ins[0].shape[1]
    for shift, ref in enumerate(ins):
        source = lax.rem(meta[CORE] + count - shift, count)
        wide[:, pl.ds(pl.multiple_of(source * size, size), size), :] = ref[...].astype(F32)
    copies = []
    for n, (tap, col) in enumerate(targets):
        window = out.at[tap, :, pl.ds(col, wide.shape[2])]
        copies.append(pltpu.make_async_copy(wide.at[n], window, sems.at[n]))
    for copy in copies:
        copy.start()
    for copy in copies:
        copy.wait()


def write_taps(device, values, targets, shape, buffer, name):
    count = len(values)
    k, rows, cols = values[0].shape
    extra = [] if buffer is None else [buffer]
    return call(
        functools.partial(write_taps_body, count, targets, len(extra)), device, (*values, *extra),
        [WHOLE] * count + [HBM] * len(extra), shape_of(shape, F32), HBM,
        scratch=[pltpu.VMEM((k, rows * count, cols), F32), pltpu.SemaphoreType.DMA((k,))],
        aliases={1 + count: 0} if extra else None, name=name,
    )


def act_body(meta, x, *acts):
    act = gelu(x[...].astype(F32)).astype(BF16)
    cols = acts[0].shape[1]
    for n, ref in enumerate(acts):
        ref[...] = act[:, n * cols : (n + 1) * cols]


def mm_parts(lefts, weight):
    cols = lefts[0].shape[1]
    return sum(mm(left[...], weight[0, n * cols : (n + 1) * cols]) for n, left in enumerate(lefts))


def mm_back_parts(lefts, weight):
    cols = lefts[0].shape[1]
    return sum(mm_back(left[...], weight[0, :, n * cols : (n + 1) * cols]) for n, left in enumerate(lefts))


def oth_out_body(meta, x0, x1, oth0, oth1, far0, far1, own0, own1, w_near, w_mid, w_far, out):
    cols = x0.shape[1]
    conv = mm_parts((oth0, oth1), w_mid) + mm_parts((far0, far1), w_near) + mm_parts((own0, own1), w_far)
    out[:, :cols] = (x0[...].astype(F32) + conv[:, :cols]).astype(BF16)
    out[:, cols:] = (x1[...].astype(F32) + conv[:, cols:]).astype(BF16)


def own_out_body(meta, x, own0, own1, oth0, oth1, far0, far1, w_near, w_mid, w_far, out):
    conv = mm_parts((own0, own1), w_mid) + mm_parts((oth0, oth1), w_near) + mm_parts((far0, far1), w_far)
    out[...] = (x[...].astype(F32) + conv).astype(BF16)


def outer_body(
    steps, count, n_extra, meta, own0, own1, oth0, oth1, far0, far1, own_far0, own_far1, u_own, u_oth, *refs
):
    extra, (keep, send, total) = refs[:n_extra], refs[n_extra:]
    i = pl.program_id(0)

    @pl.when(i == 0)
    def _():
        total[...] = jnp.zeros_like(total)

    cols = own0.shape[1]
    for n, (own, oth, far, own_far) in enumerate(((own0, oth0, far0, own_far0), (own1, oth1, far1, own_far1))):
        rows = slice(n * cols, (n + 1) * cols)
        total[0, rows] += mm_outer(own[...], u_oth[...]) + mm_outer(own_far[...], u_own[...])
        total[1, rows] += mm_outer(far[...], u_oth[...]) + mm_outer(oth[...], u_own[...])

    @pl.when(i == steps - 1)
    def _():
        lead = 0
        for part in (*extra, total):
            window = pl.ds(lead, part.shape[0])
            split_into(part, meta[CORE], count, keep.at[window], [send.at[window]])
            lead += part.shape[0]


def oth_grad_body(meta, x0, x1, u_own, oth0, oth1, far, w_near, w_mid, w_far, grad):
    cols = oth0.shape[1]
    grad_act = mm_back(u_own[...], w_near[0]) + mm_back_parts((oth0, oth1), w_mid) + mm_back(far[...], w_far[0])
    for n, (x, u) in enumerate(((x0, oth0), (x1, oth1))):
        part = slice(n * cols, (n + 1) * cols)
        _, slope = gelu_and_slope(x[...].astype(F32))
        grad[:, part] = (u[...].astype(F32) + slope * grad_act[:, part]).astype(BF16)


def own_grad_body(meta, x, u_own, oth0, oth1, far0, far1, w_near, w_mid, w_far, grad):
    _, slope = gelu_and_slope(x[...].astype(F32))
    u = u_own[...]
    grad_act = mm_back(u, w_mid[0]) + mm_back_parts((oth0, oth1), w_far) + mm_back_parts((far0, far1), w_near)
    grad[...] = (u.astype(F32) + slope * grad_act).astype(BF16)


def place_body(row, col, meta, part, buffer, out, sem):
    rows, cols = part.shape
    start = pl.multiple_of((1 - meta[SIDE]) * (buffer.shape[0] // 2), rows) + row
    copy = pltpu.make_async_copy(part, out.at[pl.ds(pl.multiple_of(start, 16), rows), pl.ds(col, cols)], sem)
    copy.start()
    copy.wait()


def place(device, part, buffer, row, col, name):
    return call(
        functools.partial(place_body, row, col), device, (part, buffer), [HBM, HBM],
        shape_of(buffer.shape, buffer.dtype), HBM, scratch=[pltpu.SemaphoreType.DMA], aliases={2: 0}, name=name,
    )


def per_device(genome, conv_weight, upstream):
    genome, upstream = genome[0], upstream[0]
    bins, chans = genome.shape
    half, cols = bins // 2, chans // 2
    block = half // 4
    steps = half // block
    count = lax.axis_size("seq")
    index = lax.axis_index("seq")
    tap = DILATION_BINS // bins
    span = 2 * tap
    dp_count, along_count = lax.axis_size("dp"), count // span
    side, along = lax.rem(index // tap, 2), index // span
    if along_count % 2 == 0:
        along = along ^ side
    def is_even(i):
        return (i // tap) % 2 == 0

    swap_pairs = [(i, i + tap if is_even(i) else i - tap) for i in range(count)]
    outer_pairs = [(i, i - span if is_even(i) else i + span) for i in range(count)]
    outer_pairs = [(i, j) for i, j in outer_pairs if 0 <= j < count]
    inner_pairs = [(j, i) for i, j in outer_pairs]

    def swap(value):
        return lax.ppermute(value, "seq", swap_pairs)

    def outward(value):
        return lax.ppermute(value, "seq", outer_pairs)

    def inward(value):
        return lax.ppermute(value, "seq", inner_pairs)

    def to_core(value, shift=1):
        return lax.ppermute(value, "seq", [(i, i - i % tap + (i % tap + shift) % tap) for i in range(count)])

    def to_dp(value, shift=1):
        return lax.ppermute(value, "dp", [(i, (i + shift) % dp_count) for i in range(dp_count)])

    flip = 1 if along_count % 2 == 0 else 0
    bits = (along_count - 1).bit_length()
    halving = along_count == 1 << bits

    def reversed_bits(value):
        return sum(((value >> n) & 1) << (bits - 1 - n) for n in range(bits)) if halving else value

    def place_along(i):
        return reversed_bits((i // span) ^ (flip * ((i // tap) % 2)))

    def device_at(i, side, position):
        return (reversed_bits(position) ^ (flip * side)) * span + side * tap + i % tap

    def to_along(value, move):
        pairs = [(i, device_at(i, (i // tap) % 2, move(place_along(i)))) for i in range(count)]
        return lax.ppermute(value, "seq", pairs)

    def to_side(value):
        pairs = [(i, device_at(i, 1 - (i // tap) % 2, place_along(i))) for i in range(count)]
        return lax.ppermute(value, "seq", pairs)

    rows_spec = pl.BlockSpec((block, chans), lambda i, s: (i, 0))
    own_spec = pl.BlockSpec((block, chans), lambda i, s: (s[SIDE] * steps + i, 0))
    w_near = pl.BlockSpec((1, chans, chans), lambda i, s: (2 - 2 * s[SIDE], 0, 0))
    w_mid = pl.BlockSpec((1, chans, chans), lambda i, s: (1, 0, 0))
    w_far = pl.BlockSpec((1, chans, chans), lambda i, s: (2 * s[SIDE], 0, 0))
    half_shape, whole_shape = shape_of((half, chans), BF16), shape_of((bins, chans), BF16)
    along = reversed_bits(along)
    along_bits = [(along >> n) & 1 for n in reversed(range(bits))]
    meta = jnp.stack([side, lax.rem(index, tap), lax.axis_index("dp"), along, *along_bits]).astype(jnp.int32)
    device = Device(meta)

    part_spec = pl.BlockSpec((block, cols), lambda i, s: (i, 0))
    weights, weight_specs = (conv_weight,) * 3, [w_near, w_mid, w_far]

    staged = halving and (chans // tap // dp_count) % (16 * along_count) == 0

    def core_stage(parts, name, after=()):
        keep, send = parts
        keep, send = reduce(device, [[keep, to_core(send)]], dp_count, DP, dtype=BF16, name=name + "_core", after=after)
        return [keep, to_dp(send)]

    def along_stage(groups, step, after=()):
        if not staged:
            return reduce(device, groups, name=f"along{step}", after=after)
        keep, send = reduce(device, groups, 2, ALONG_BITS + step, dtype=BF16, name=f"along{step}", after=after)
        return [keep, to_along(send, lambda position: position ^ (1 << (bits - 1 - step)))]

    def side_stage(groups, after=()):
        (total,) = reduce(device, groups, swap_from=2, name="last", after=after)
        if not staged:
            together = [[i + span * j for j in range(along_count)] for i in range(span)]
            total = lax.psum(total, "seq", axis_index_groups=together)
        return [total, to_side(total)]

    def round_and_spread(parts, after=()):
        (total,) = reduce(device, [parts], dtype=BF16, name="side", after=after)
        moves = [lambda position, s=s: (position + s) % along_count for s in range(1, along_count)]
        return [total] + [to_along(total, move) for move in moves if staged]

    def gather_along(parts):
        total = gather(device, parts, ALONG, "all_along") if staged else parts[0]
        return [total] + [to_dp(total, s) for s in range(1, dp_count)]

    def gather_dp(parts):
        total = gather(device, parts, DP, "all_dp")
        return [total] + [to_core(total, s) for s in range(1, tap)]

    def outer_taps(k, extra=(), dtype=F32):
        u_own_spec = pl.BlockSpec((block, cols), lambda i, s: (i, k))
        piece = (2 + sum(part.shape[0] for part in extra), chans // tap, cols)
        return call(
            functools.partial(outer_body, steps, tap, len(extra)), device,
            (*a_own, *a_oth, *a_oth_far, *a_own_far, u_own, u_oth[k], *extra),
            [*[part_spec] * 8, u_own_spec, part_spec, *[WHOLE] * len(extra)], [shape_of(piece, F32), shape_of(piece, dtype)],
            [pl.BlockSpec(piece, lambda i, s: (0, 0, 0))] * 2, grid=(steps,),
            scratch=[pltpu.VMEM((2, chans, cols), F32)], name=f"outer_taps{k}",
        )

    def oth_act(x, name):
        return call(
            act_body, device, (x,), [part_spec], shape_of((half, cols), BF16), part_spec, grid=(steps,), name=name
        )

    (x_send0,) = cut(device, (genome,), [(0, False, 0, half, cols)], "cut_first")
    x_oth0 = swap(x_send0)
    a_own = call(
        act_body, device, (genome,), [own_spec], [shape_of((half, cols), BF16)] * 2, [part_spec] * 2, grid=(steps,),
        name="own_act",
    )
    a_oth_far = [outward(part) for part in a_own]
    x_send1, u_send0, u_send1, u_own = cut(
        device, (genome, upstream),
        [(0, False, cols, half, cols), (1, False, 0, half, cols), (1, False, cols, half, cols), (1, True, 0, half, chans)],
        "cut_rest",
    )
    x_oth1, u_oth = swap(x_send1), [swap(u_send0), swap(u_send1)]
    u_oth_far = outward(u_own)

    mid = call(
        lambda meta, *refs: mid_body(*refs), device, (genome, upstream), [rows_spec] * 2,
        shape_of((2, chans, cols), F32), pl.BlockSpec((2, chans, cols), lambda i, s: (0, 0, 0)), grid=(2 * steps,),
        name="mid_tap",
    )
    a_oth0 = oth_act(x_oth0, "oth_act0")
    a_own_far0 = inward(a_oth0)
    a_oth1 = oth_act(x_oth1, "oth_act1")
    a_own_far1 = inward(a_oth1)
    a_oth, a_own_far = [a_oth0, a_oth1], [a_own_far0, a_own_far1]
    out = call(
        oth_out_body, device, (x_oth0, x_oth1, *a_oth, *a_oth_far, *a_own, *weights),
        [*[part_spec] * 8, *weight_specs], half_shape, rows_spec, grid=(steps,), name="oth_out", after=(a_own_far[0],),
    )
    out = swap(out)
    outer0 = outer_taps(0, [mid], BF16)
    u_own_far0 = inward(u_oth[0])
    outer1 = outer_taps(1)
    u_own_far1 = inward(u_oth[1])
    outer0 = core_stage(outer0, "outer0", after=(u_own_far0,))
    outer1 = core_stage(outer1, "outer1")
    grad = call(
        oth_grad_body, device, (x_oth0, x_oth1, u_own, *u_oth, u_oth_far, *weights),
        [part_spec, part_spec, rows_spec, part_spec, part_spec, rows_spec, *weight_specs], half_shape, rows_spec,
        grid=(steps,), name="oth_grad",
    )
    grad = swap(grad)
    output = call(
        own_out_body, device, (genome, *a_own, *a_oth, *a_own_far, *weights),
        [own_spec, *[part_spec] * 6, *weight_specs], whole_shape, own_spec, grid=(steps,), name="own_out",
    )
    parts = along_stage([outer0, outer1], 0)
    grad_genome = call(
        own_grad_body, device, (genome, u_own, *u_oth, u_own_far0, u_own_far1, *weights),
        [own_spec, rows_spec, *[part_spec] * 4, *weight_specs], whole_shape, own_spec, grid=(steps,), name="own_grad",
    )
    parts = along_stage([parts], 1)
    output = place(device, out, output, 0, 0, "place_out")
    parts = side_stage([parts])
    parts = round_and_spread(parts)
    parts = gather_along(parts)
    grad_genome = place(device, grad, grad_genome, 0, 0, "place_grad")
    parts = gather_dp(parts)
    targets = [(1, 0), (1, cols), (0, 0), (2, 0), (0, cols), (2, cols)]
    grad_weight = write_taps(device, parts, targets, conv_weight.shape, None, "write_taps")
    return (output[None], grad_genome[None], grad_weight)


def solution(mesh):
    return jax.shard_map(
        per_device,
        mesh=mesh,
        in_specs=(P("dp", "seq", None), P(), P("dp", "seq", None)),
        out_specs=(P("dp", "seq", None), P("dp", "seq", None), P()),
        check_vma=False,
    )
```

```python
import functools

import jax
import jax.numpy as jnp
from jax import lax
from jax.experimental import pallas as pl
from jax.experimental.pallas import tpu as pltpu
from jax.sharding import PartitionSpec as P

DILATION_BINS = 4096
BF16, F32 = jnp.bfloat16, jnp.float32
VMEM_BYTES = 40 * 1024 * 1024
COSTS = {}
SIDE, CORE, DP, ALONG, ALONG_BITS = range(5)
HBM = pl.BlockSpec(memory_space=pltpu.HBM)
WHOLE = pl.BlockSpec(memory_space=pltpu.VMEM)


def shape_of(shape, dtype):
    return jax.ShapeDtypeStruct(shape, dtype)


TOKEN = jax.ShapeDtypeStruct((8, 128), F32)


class Device:
    def __init__(self, meta):
        self.meta, self.token = meta, None


def call(
    body, device, operands, in_specs, outs, out_specs, grid=(), scratch=(), aliases=None, name=None, after=()
):
    first = device.token is None
    n_in, single = len(operands), not isinstance(outs, list)
    outs, out_specs = ([outs], [out_specs]) if single else (outs, out_specs)
    n_out = len(outs)
    tokens = [*after] if first else [device.token, *after]

    def chained(meta, *refs):
        rest = refs[n_in + len(tokens) :]
        body(meta, *refs[:n_in], *rest[:n_out], *rest[n_out + 1 :])

    results = pl.pallas_call(
        chained,
        grid_spec=pltpu.PrefetchScalarGridSpec(
            num_scalar_prefetch=1, grid=grid, in_specs=[*in_specs, *[HBM] * len(tokens)], out_specs=[*out_specs, HBM],
            scratch_shapes=list(scratch),
        ),
        out_shape=[*outs, TOKEN],
        input_output_aliases=aliases or {},
        compiler_params=pltpu.CompilerParams(vmem_limit_bytes=VMEM_BYTES),
        cost_estimate=pl.CostEstimate(flops=1, bytes_accessed=COSTS.get(name, 200_000), transcendentals=0),
        name=name,
    )(device.meta, *operands, *tokens)
    device.token = results[-1]
    return results[0] if single else results[:-1]


def gelu_parts(x):
    k = 0.7978845608028654
    square = x * x
    t = jnp.tanh(k * (x * (1.0 + 0.044715 * square)))
    return t, square, k


def gelu(x):
    t, _, _ = gelu_parts(x)
    return x * (0.5 * (1.0 + t))


def gelu_and_slope(x):
    t, square, k = gelu_parts(x)
    cdf = 0.5 * (1.0 + t)
    slope = cdf + 0.5 * x * (1.0 - t * t) * (k + (3 * 0.044715 * k) * square)
    return x * cdf, slope


def mm(left, right):
    return lax.dot_general(left, right, (((1,), (0,)), ((), ())), preferred_element_type=F32)


def mm_back(left, right):
    return lax.dot_general(left, right, (((1,), (1,)), ((), ())), preferred_element_type=F32)


def mm_outer(left, right):
    return lax.dot_general(left, right, (((0,), (0,)), ((), ())), preferred_element_type=F32)


def cut_body(plan, n_in, meta, *refs):
    ins, outs, sems = refs[:n_in], refs[n_in:-1], refs[-1]
    copies = []
    for n, (which, own, col, rows, cols) in enumerate(plan):
        start = (meta[SIDE] if own else 1 - meta[SIDE]) * rows
        window = ins[which].at[pl.ds(pl.multiple_of(start, rows), rows), pl.ds(col, cols)]
        copies.append(pltpu.make_async_copy(window, outs[n], sems.at[n]))
    for copy in copies:
        copy.start()
    for copy in copies:
        copy.wait()


def cut(device, operands, plan, name):
    outs = [shape_of((rows, cols), BF16) for _, _, _, rows, cols in plan]
    return call(
        functools.partial(cut_body, plan, len(operands)), device, operands, [HBM] * len(operands), outs,
        [HBM] * len(plan), scratch=[pltpu.SemaphoreType.DMA((len(plan),))], name=name,
    )


def split_into(total, position, count, keep, sends):
    size = total.shape[1] // count
    for shift, ref in enumerate((keep, *sends)):
        there = lax.rem(position + shift, count)
        ref[...] = total[:, pl.ds(pl.multiple_of(there * size, size), size), :].astype(ref.dtype)


def mid_body(x, u, total):
    @pl.when(pl.program_id(0) == 0)
    def _():
        total[...] = jnp.zeros_like(total)

    cols = total.shape[2]
    product = mm_outer(gelu(x[...].astype(F32)).astype(BF16), u[...])
    for part in range(2):
        total[part] += product[:, part * cols : (part + 1) * cols]


def reduce_body(sizes, n_out, place, swap_from, meta, *refs):
    ins, outs, total = refs[: sum(sizes)], refs[sum(sizes) : -1], refs[-1]
    first = lead = 0
    for size in sizes:
        value = ins[first][...].astype(F32)
        for ref in ins[first + 1 : first + size]:
            value = value + ref[...].astype(F32)
        total[lead : lead + value.shape[0]] = value
        first, lead = first + size, lead + value.shape[0]
    for part in range(swap_from, lead, 2):
        pair = total[part : part + 2]
        for n in range(2):
            total[part + n] = jnp.where(meta[SIDE] == 0, pair[n], pair[1 - n])
    if n_out > 1:
        split_into(total, meta[place], n_out, outs[0], outs[1:])
    else:
        outs[0][...] = total[...].astype(outs[0].dtype)


def reduce(device, groups, n_out=1, place=None, swap_from=None, dtype=F32, name=None, after=()):
    _, rows, cols = groups[0][0].shape
    k = sum(group[0].shape[0] for group in groups)
    values = [value for group in groups for value in group]
    dtypes = [dtype] if n_out == 1 else [F32] + [dtype] * (n_out - 1)
    outs = [shape_of((k, rows // n_out, cols), each) for each in dtypes]
    sizes = [len(group) for group in groups]
    body = functools.partial(reduce_body, sizes, n_out, place, k if swap_from is None else swap_from)
    return call(
        body, device, values, [WHOLE] * len(values), outs, [WHOLE] * n_out,
        scratch=[pltpu.VMEM((k, rows, cols), F32)], name=name, after=after,
    )


def gather_body(count, place, meta, *refs):
    ins, out = refs[:count], refs[count]
    size = ins[0].shape[1]
    for shift, ref in enumerate(ins):
        source = lax.rem(meta[place] + count - shift, count)
        out[:, pl.ds(pl.multiple_of(source * size, size), size), :] = ref[...]


def gather(device, values, place, name=None, after=()):
    count = len(values)
    k, rows, cols = values[0].shape
    return call(
        functools.partial(gather_body, count, place), device, values, [WHOLE] * count,
        shape_of((k, rows * count, cols), BF16), WHOLE, name=name, after=after,
    )


def write_taps_body(shifts, groups, targets, aliased, meta, *refs):
    parts = refs[: len(shifts)]
    out, wide, sems = refs[len(shifts) + aliased :]
    rows, cols = parts[0].shape[1:]
    cores, dps = groups
    copies = []
    for m, (part, (core_shift, dp_shift)) in enumerate(zip(parts, shifts)):
        core = lax.rem(meta[CORE] + cores - core_shift, cores)
        dp = lax.rem(meta[DP] + dps - dp_shift, dps)
        first = pl.multiple_of((core * dps + dp) * rows, rows)
        wide[m] = part[...].astype(F32)
        for n, (tap, col) in enumerate(targets):
            window = out.at[tap, pl.ds(first, rows), pl.ds(col, cols)]
            copy = pltpu.make_async_copy(wide.at[m, n], window, sems.at[m, n])
            copy.start()
            copies.append(copy)
    for copy in copies:
        copy.wait()


def write_taps(device, parts, shifts, groups, targets, shape, buffer, name, after=()):
    extra = [] if buffer is None else [buffer]
    return call(
        functools.partial(write_taps_body, shifts, groups, targets, len(extra)), device, (*parts, *extra),
        [WHOLE] * len(parts) + [HBM] * len(extra), shape_of(shape, F32), HBM,
        scratch=[
            pltpu.VMEM((len(parts), *parts[0].shape), F32), pltpu.SemaphoreType.DMA((len(parts), len(targets)))
        ],
        aliases={1 + len(parts): 0} if extra else None, name=name, after=after,
    )


def act_body(meta, x, *acts):
    act = gelu(x[...].astype(F32)).astype(BF16)
    cols = acts[0].shape[1]
    for n, ref in enumerate(acts):
        ref[...] = act[:, n * cols : (n + 1) * cols]


def mm_parts(lefts, weight):
    cols = lefts[0].shape[1]
    return sum(mm(left[...], weight[0, n * cols : (n + 1) * cols]) for n, left in enumerate(lefts))


def mm_back_parts(lefts, weight):
    cols = lefts[0].shape[1]
    return sum(mm_back(left[...], weight[0, :, n * cols : (n + 1) * cols]) for n, left in enumerate(lefts))


def oth_out_body(meta, x0, x1, oth0, oth1, far0, far1, own0, own1, w_near, w_mid, w_far, out):
    cols = x0.shape[1]
    conv = mm_parts((oth0, oth1), w_mid) + mm_parts((far0, far1), w_near) + mm_parts((own0, own1), w_far)
    out[:, :cols] = (x0[...].astype(F32) + conv[:, :cols]).astype(BF16)
    out[:, cols:] = (x1[...].astype(F32) + conv[:, cols:]).astype(BF16)


def own_out_body(meta, x, own0, own1, oth0, oth1, far0, far1, w_near, w_mid, w_far, out):
    conv = mm_parts((own0, own1), w_mid) + mm_parts((oth0, oth1), w_near) + mm_parts((far0, far1), w_far)
    out[...] = (x[...].astype(F32) + conv).astype(BF16)


def outer_first_body(steps, count, meta, own0, own1, oth0, oth1, far0, far1, own_far0, own_far1, u_own, u_oth, mid, *refs):
    keep, send, rest, total = refs
    i = pl.program_id(0)

    @pl.when(i == 0)
    def _():
        total[...] = jnp.zeros_like(total)
        rest[...] = jnp.zeros_like(rest)

    cols = own0.shape[1]
    for n, (own, oth, far, own_far) in enumerate(((own0, oth0, far0, own_far0), (own1, oth1, far1, own_far1))):
        rows = slice(n * cols, (n + 1) * cols)
        u_first, u_second = u_own[:, :cols], u_own[:, cols:]
        total[0, rows] += mm_outer(own[...], u_oth[...]) + mm_outer(own_far[...], u_first)
        total[1, rows] += mm_outer(far[...], u_oth[...]) + mm_outer(oth[...], u_first)
        rest[0, rows] += mm_outer(own_far[...], u_second)
        rest[1, rows] += mm_outer(oth[...], u_second)

    @pl.when(i == steps - 1)
    def _():
        lead = 0
        for part in (mid, total):
            window = pl.ds(lead, part.shape[0])
            split_into(part, meta[CORE], count, keep.at[window], [send.at[window]])
            lead += part.shape[0]


def outer_second_body(steps, count, meta, own0, own1, far0, far1, u_oth, rest, keep, send, total):
    i = pl.program_id(0)

    @pl.when(i == 0)
    def _():
        total[...] = rest[...]

    cols = own0.shape[1]
    for n, (own, far) in enumerate(((own0, far0), (own1, far1))):
        rows = slice(n * cols, (n + 1) * cols)
        total[0, rows] += mm_outer(own[...], u_oth[...])
        total[1, rows] += mm_outer(far[...], u_oth[...])

    @pl.when(i == steps - 1)
    def _():
        split_into(total, meta[CORE], count, keep, [send])


def oth_grad_body(meta, x0, x1, u_own, oth0, oth1, far, w_near, w_mid, w_far, grad):
    cols = oth0.shape[1]
    grad_act = mm_back(u_own[...], w_near[0]) + mm_back_parts((oth0, oth1), w_mid) + mm_back(far[...], w_far[0])
    for n, (x, u) in enumerate(((x0, oth0), (x1, oth1))):
        part = slice(n * cols, (n + 1) * cols)
        _, slope = gelu_and_slope(x[...].astype(F32))
        grad[:, part] = (u[...].astype(F32) + slope * grad_act[:, part]).astype(BF16)


def own_grad_body(meta, x, u_own, oth0, oth1, far0, far1, w_near, w_mid, w_far, grad):
    _, slope = gelu_and_slope(x[...].astype(F32))
    u = u_own[...]
    grad_act = mm_back(u, w_mid[0]) + mm_back_parts((oth0, oth1), w_far) + mm_back_parts((far0, far1), w_near)
    grad[...] = (u.astype(F32) + slope * grad_act).astype(BF16)


def place_body(row, col, meta, part, buffer, out, sem):
    rows, cols = part.shape
    start = pl.multiple_of((1 - meta[SIDE]) * (buffer.shape[0] // 2), rows) + row
    copy = pltpu.make_async_copy(part, out.at[pl.ds(pl.multiple_of(start, 16), rows), pl.ds(col, cols)], sem)
    copy.start()
    copy.wait()


def place(device, part, buffer, row, col, name, after=()):
    return call(
        functools.partial(place_body, row, col), device, (part, buffer), [HBM, HBM],
        shape_of(buffer.shape, buffer.dtype), HBM, scratch=[pltpu.SemaphoreType.DMA], aliases={2: 0}, name=name, after=after,
    )


def per_device(genome, conv_weight, upstream):
    genome, upstream = genome[0], upstream[0]
    bins, chans = genome.shape
    half, cols = bins // 2, chans // 2
    block = half // 4
    steps = half // block
    count = lax.axis_size("seq")
    index = lax.axis_index("seq")
    tap = DILATION_BINS // bins
    span = 2 * tap
    dp_count, along_count = lax.axis_size("dp"), count // span
    side, along = lax.rem(index // tap, 2), index // span
    if along_count % 2 == 0:
        along = along ^ side
    def is_even(i):
        return (i // tap) % 2 == 0

    swap_pairs = [(i, i + tap if is_even(i) else i - tap) for i in range(count)]
    outer_pairs = [(i, i - span if is_even(i) else i + span) for i in range(count)]
    outer_pairs = [(i, j) for i, j in outer_pairs if 0 <= j < count]
    inner_pairs = [(j, i) for i, j in outer_pairs]

    def swap(value):
        return lax.ppermute(value, "seq", swap_pairs)

    def outward(value):
        return lax.ppermute(value, "seq", outer_pairs)

    def inward(value):
        return lax.ppermute(value, "seq", inner_pairs)

    def to_core(value, shift=1):
        return lax.ppermute(value, "seq", [(i, i - i % tap + (i % tap + shift) % tap) for i in range(count)])

    def to_dp(value, shift=1):
        return lax.ppermute(value, "dp", [(i, (i + shift) % dp_count) for i in range(dp_count)])

    flip = 1 if along_count % 2 == 0 else 0
    bits = (along_count - 1).bit_length()
    halving = along_count == 1 << bits

    def reversed_bits(value):
        return sum(((value >> n) & 1) << (bits - 1 - n) for n in range(bits)) if halving else value

    def place_along(i):
        return reversed_bits((i // span) ^ (flip * ((i // tap) % 2)))

    def device_at(i, side, position):
        return (reversed_bits(position) ^ (flip * side)) * span + side * tap + i % tap

    def to_along(value, move):
        pairs = [(i, device_at(i, (i // tap) % 2, move(place_along(i)))) for i in range(count)]
        return lax.ppermute(value, "seq", pairs)

    def to_side(value):
        pairs = [(i, device_at(i, 1 - (i // tap) % 2, place_along(i))) for i in range(count)]
        return lax.ppermute(value, "seq", pairs)

    rows_spec = pl.BlockSpec((block, chans), lambda i, s: (i, 0))
    own_spec = pl.BlockSpec((block, chans), lambda i, s: (s[SIDE] * steps + i, 0))
    w_near = pl.BlockSpec((1, chans, chans), lambda i, s: (2 - 2 * s[SIDE], 0, 0))
    w_mid = pl.BlockSpec((1, chans, chans), lambda i, s: (1, 0, 0))
    w_far = pl.BlockSpec((1, chans, chans), lambda i, s: (2 * s[SIDE], 0, 0))
    half_shape, whole_shape = shape_of((half, chans), BF16), shape_of((bins, chans), BF16)
    along = reversed_bits(along)
    along_bits = [(along >> n) & 1 for n in reversed(range(bits))]
    meta = jnp.stack([side, lax.rem(index, tap), lax.axis_index("dp"), along, *along_bits]).astype(jnp.int32)
    device = Device(meta)

    part_spec = pl.BlockSpec((block, cols), lambda i, s: (i, 0))
    weights, weight_specs = (conv_weight,) * 3, [w_near, w_mid, w_far]

    staged = halving and (chans // tap // dp_count) % (16 * along_count) == 0

    def core_stage(parts, name, after=()):
        keep, send = parts
        keep, send = reduce(device, [[keep, to_core(send)]], dp_count, DP, dtype=BF16, name=name + "_core", after=after)
        return [keep, to_dp(send)]

    def along_stage(groups, step, after=()):
        if not staged:
            return reduce(device, groups, name=f"along{step}", after=after)
        keep, send = reduce(device, groups, 2, ALONG_BITS + step, dtype=BF16, name=f"along{step}", after=after)
        return [keep, to_along(send, lambda position: position ^ (1 << (bits - 1 - step)))]

    def side_stage(groups, after=()):
        (total,) = reduce(device, groups, swap_from=2, name="last", after=after)
        if not staged:
            together = [[i + span * j for j in range(along_count)] for i in range(span)]
            total = lax.psum(total, "seq", axis_index_groups=together)
        return [total, to_side(total)]

    def round_and_spread(parts, after=()):
        (total,) = reduce(device, [parts], dtype=BF16, name="side", after=after)
        moves = [lambda position, s=s: (position + s) % along_count for s in range(1, along_count)]
        return [total] + [to_along(total, move) for move in moves if staged]

    def join(pieces, name, after=()):
        total = gather(device, pieces, ALONG, name, after) if staged else pieces[0]
        return [total] + [to_core(total, s) for s in range(1, tap)]

    targets = [(1, 0), (1, cols), (0, 0), (2, 0), (0, cols), (2, cols)]

    def write(joined, dp_shift, buffer, after=()):
        shifts = [(core_shift, dp_shift) for core_shift in range(tap)]
        return write_taps(
            device, joined, shifts, (tap, dp_count), targets, conv_weight.shape, buffer, f"write_taps{dp_shift}", after
        )

    def slices_of(parts, dtype):
        piece = (parts, chans // tap, cols)
        return [shape_of(piece, F32), shape_of(piece, dtype)], [pl.BlockSpec(piece, lambda i, s: (0, 0, 0))] * 2

    sums_shape = (2, chans, cols)
    sums_spec = pl.BlockSpec(sums_shape, lambda i, s: (0, 0, 0))

    def oth_act(x, name, after=()):
        return call(
            act_body, device, (x,), [part_spec], shape_of((half, cols), BF16), part_spec, grid=(steps,), name=name,
            after=after,
        )

    (x_send0,) = cut(device, (genome,), [(0, False, 0, half, cols)], "cut_first")
    x_oth0 = swap(x_send0)
    a_own = call(
        act_body, device, (genome,), [own_spec], [shape_of((half, cols), BF16)] * 2, [part_spec] * 2, grid=(steps,),
        name="own_act",
    )
    a_oth_far = [outward(part) for part in a_own]
    x_send1, u_send0, u_send1, u_own = cut(
        device, (genome, upstream),
        [(0, False, cols, half, cols), (1, False, 0, half, cols), (1, False, cols, half, cols), (1, True, 0, half, chans)],
        "cut_rest",
    )
    x_oth1, u_oth = swap(x_send1), [swap(u_send0), swap(u_send1)]
    u_oth_far, u_own_far = outward(u_own), [inward(part) for part in u_oth]
    mid = call(
        lambda meta, *refs: mid_body(*refs), device, (genome, upstream), [rows_spec] * 2, shape_of(sums_shape, F32),
        sums_spec, grid=(2 * steps,), name="mid_tap",
    )
    a_oth0 = oth_act(x_oth0, "oth_act0")
    a_own_far0 = inward(a_oth0)
    a_oth1 = oth_act(x_oth1, "oth_act1")
    a_own_far1 = inward(a_oth1)
    out = call(
        oth_out_body, device, (x_oth0, x_oth1, a_oth0, a_oth1, *a_oth_far, *a_own, *weights),
        [*[part_spec] * 8, *weight_specs], half_shape, rows_spec, grid=(steps,), name="oth_out", after=(a_own_far0,),
    )
    out = swap(out)
    slices, specs = slices_of(4, BF16)
    *outer0, rest = call(
        functools.partial(outer_first_body, steps, tap), device,
        (*a_own, a_oth0, a_oth1, *a_oth_far, a_own_far0, a_own_far1, u_own, u_oth[0], mid),
        [*[part_spec] * 8, rows_spec, part_spec, WHOLE], [*slices, shape_of(sums_shape, F32)], [*specs, sums_spec],
        grid=(steps,), scratch=[pltpu.VMEM(sums_shape, F32)], name="outer_first",
    )
    slices, specs = slices_of(2, F32)
    outer1 = call(
        functools.partial(outer_second_body, steps, tap), device, (*a_own, *a_oth_far, u_oth[1], rest),
        [*[part_spec] * 5, WHOLE], slices, specs, grid=(steps,), scratch=[pltpu.VMEM(sums_shape, F32)],
        name="outer_second",
    )
    outer0 = core_stage(outer0, "outer0", after=(u_own_far[0],))
    outer1 = core_stage(outer1, "outer1")
    grad = call(
        oth_grad_body, device, (x_oth0, x_oth1, u_own, *u_oth, u_oth_far, *weights),
        [part_spec, part_spec, rows_spec, part_spec, part_spec, rows_spec, *weight_specs], half_shape, rows_spec,
        grid=(steps,), name="oth_grad",
    )
    grad = swap(grad)
    parts = along_stage([outer0, outer1], 0)
    output = call(
        own_out_body, device, (genome, *a_own, a_oth0, a_oth1, a_own_far0, a_own_far1, *weights),
        [own_spec, *[part_spec] * 6, *weight_specs], whole_shape, own_spec, grid=(steps,), name="own_out",
    )
    output = place(device, out, output, 0, 0, "place_out")
    parts = along_stage([parts], 1)
    grad_genome = call(
        own_grad_body, device, (genome, u_own, *u_oth, *u_own_far, *weights),
        [own_spec, rows_spec, *[part_spec] * 4, *weight_specs], whole_shape, own_spec, grid=(steps,), name="own_grad",
    )
    parts = side_stage([parts])
    pieces = round_and_spread(parts)
    far_pieces = [[to_dp(piece, s) for piece in pieces] for s in range(1, dp_count)]
    joined = join(pieces, "join")
    joined_far = [join(far, f"join_far{s}") for s, far in enumerate(far_pieces, 1)]
    grad_genome = place(device, grad, grad_genome, 0, 0, "place_grad")
    grad_weight = write(joined, 0, None)
    for s, far in enumerate(joined_far, 1):
        grad_weight = write(far, s, grad_weight)
    return (output[None], grad_genome[None], grad_weight)


def solution(mesh):
    return jax.shard_map(
        per_device,
        mesh=mesh,
        in_specs=(P("dp", "seq", None), P(), P("dp", "seq", None)),
        out_specs=(P("dp", "seq", None), P("dp", "seq", None), P()),
        check_vma=False,
    )
```

```python
import functools

import jax
import jax.numpy as jnp
from jax import lax
from jax.experimental import pallas as pl
from jax.experimental.pallas import tpu as pltpu
from jax.sharding import PartitionSpec as P

DILATION_BINS = 4096
BF16, F32 = jnp.bfloat16, jnp.float32
VMEM_BYTES = 40 * 1024 * 1024
SIDE, CORE, DP, ALONG, ALONG_BITS = range(5)
HBM = pl.BlockSpec(memory_space=pltpu.HBM)
WHOLE = pl.BlockSpec(memory_space=pltpu.VMEM)


def shape_of(shape, dtype):
    return jax.ShapeDtypeStruct(shape, dtype)


TOKEN = jax.ShapeDtypeStruct((8, 128), F32)


class Device:
    def __init__(self, meta):
        self.meta, self.token = meta, None


def call(
    body, device, operands, in_specs, outs, out_specs, grid=(), scratch=(), aliases=None, name=None, after=()
):
    first = device.token is None
    n_in, single = len(operands), not isinstance(outs, list)
    outs, out_specs = ([outs], [out_specs]) if single else (outs, out_specs)
    n_out = len(outs)
    tokens = [*after] if first else [device.token, *after]

    def chained(meta, *refs):
        rest = refs[n_in + len(tokens) :]
        body(meta, *refs[:n_in], *rest[:n_out], *rest[n_out + 1 :])

    results = pl.pallas_call(
        chained,
        grid_spec=pltpu.PrefetchScalarGridSpec(
            num_scalar_prefetch=1, grid=grid, in_specs=[*in_specs, *[HBM] * len(tokens)], out_specs=[*out_specs, HBM],
            scratch_shapes=list(scratch),
        ),
        out_shape=[*outs, TOKEN],
        input_output_aliases=aliases or {},
        compiler_params=pltpu.CompilerParams(vmem_limit_bytes=VMEM_BYTES),
        cost_estimate=pl.CostEstimate(flops=1, bytes_accessed=200_000, transcendentals=0),
        name=name,
    )(device.meta, *operands, *tokens)
    device.token = results[-1]
    return results[0] if single else results[:-1]


def gelu_parts(x):
    k = 0.7978845608028654
    square = x * x
    t = jnp.tanh(k * (x * (1.0 + 0.044715 * square)))
    return t, square, k


def gelu(x):
    t, _, _ = gelu_parts(x)
    return x * (0.5 * (1.0 + t))


def gelu_and_slope(x):
    t, square, k = gelu_parts(x)
    cdf = 0.5 * (1.0 + t)
    slope = cdf + 0.5 * x * (1.0 - t * t) * (k + (3 * 0.044715 * k) * square)
    return x * cdf, slope


def mm(left, right):
    return lax.dot_general(left, right, (((1,), (0,)), ((), ())), preferred_element_type=F32)


def mm_back(left, right):
    return lax.dot_general(left, right, (((1,), (1,)), ((), ())), preferred_element_type=F32)


def mm_outer(left, right):
    return lax.dot_general(left, right, (((0,), (0,)), ((), ())), preferred_element_type=F32)


def cut_body(plan, n_in, meta, *refs):
    ins, outs, sems = refs[:n_in], refs[n_in:-1], refs[-1]
    copies = []
    for n, (which, own, col, rows, cols) in enumerate(plan):
        start = (meta[SIDE] if own else 1 - meta[SIDE]) * rows
        window = ins[which].at[pl.ds(pl.multiple_of(start, rows), rows), pl.ds(col, cols)]
        copies.append(pltpu.make_async_copy(window, outs[n], sems.at[n]))
    for copy in copies:
        copy.start()
    for copy in copies:
        copy.wait()


def cut(device, operands, plan, name):
    outs = [shape_of((rows, cols), BF16) for _, _, _, rows, cols in plan]
    return call(
        functools.partial(cut_body, plan, len(operands)), device, operands, [HBM] * len(operands), outs,
        [HBM] * len(plan), scratch=[pltpu.SemaphoreType.DMA((len(plan),))], name=name,
    )


def split_into(total, position, count, keep, sends):
    size = total.shape[1] // count
    for shift, ref in enumerate((keep, *sends)):
        there = lax.rem(position + shift, count)
        ref[...] = total[:, pl.ds(pl.multiple_of(there * size, size), size), :].astype(ref.dtype)


def mid_body(x, u, total):
    @pl.when(pl.program_id(0) == 0)
    def _():
        total[...] = jnp.zeros_like(total)

    cols = total.shape[2]
    product = mm_outer(gelu(x[...].astype(F32)).astype(BF16), u[...])
    for part in range(2):
        total[part] += product[:, part * cols : (part + 1) * cols]


def reduce_body(sizes, n_out, place, swap_from, meta, *refs):
    ins, outs, total = refs[: sum(sizes)], refs[sum(sizes) : -1], refs[-1]
    first = lead = 0
    for size in sizes:
        value = ins[first][...].astype(F32)
        for ref in ins[first + 1 : first + size]:
            value = value + ref[...].astype(F32)
        total[lead : lead + value.shape[0]] = value
        first, lead = first + size, lead + value.shape[0]
    for part in range(swap_from, lead, 2):
        pair = total[part : part + 2]
        for n in range(2):
            total[part + n] = jnp.where(meta[SIDE] == 0, pair[n], pair[1 - n])
    if n_out > 1:
        split_into(total, meta[place], n_out, outs[0], outs[1:])
    else:
        outs[0][...] = total[...].astype(outs[0].dtype)


def reduce(device, groups, n_out=1, place=None, swap_from=None, dtype=F32, name=None, after=()):
    _, rows, cols = groups[0][0].shape
    k = sum(group[0].shape[0] for group in groups)
    values = [value for group in groups for value in group]
    dtypes = [dtype] if n_out == 1 else [F32] + [dtype] * (n_out - 1)
    outs = [shape_of((k, rows // n_out, cols), each) for each in dtypes]
    sizes = [len(group) for group in groups]
    body = functools.partial(reduce_body, sizes, n_out, place, k if swap_from is None else swap_from)
    return call(
        body, device, values, [WHOLE] * len(values), outs, [WHOLE] * n_out,
        scratch=[pltpu.VMEM((k, rows, cols), F32)], name=name, after=after,
    )


def gather_body(count, place, meta, *refs):
    ins, out = refs[:count], refs[count]
    size = ins[0].shape[1]
    for shift, ref in enumerate(ins):
        source = lax.rem(meta[place] + count - shift, count)
        out[:, pl.ds(pl.multiple_of(source * size, size), size), :] = ref[...]


def gather(device, values, place, name=None, after=()):
    count = len(values)
    k, rows, cols = values[0].shape
    return call(
        functools.partial(gather_body, count, place), device, values, [WHOLE] * count,
        shape_of((k, rows * count, cols), BF16), WHOLE, name=name, after=after,
    )


def returned_copy(meta, part, out, sem):
    rows = part.shape[0]
    start = pl.multiple_of((1 - meta[SIDE]) * rows, rows)
    return pltpu.make_async_copy(part, out.at[pl.ds(start, rows)], sem)


def write_taps_body(shifts, groups, targets, aliased, placing, meta, *refs):
    parts, refs = refs[: len(shifts)], refs[len(shifts) :]
    returned, refs = refs[: 2 * placing], refs[2 * placing + aliased :]
    out, wide, sems = refs[0], refs[-2 - placing], refs[-1 - placing]
    rows, cols = parts[0].shape[1:]
    cores, dps = groups
    copies = []
    if placing:
        copies.append(returned_copy(meta, returned[0], refs[1], refs[-1]))
        copies[0].start()
    for m, (part, (core_shift, dp_shift)) in enumerate(zip(parts, shifts)):
        core = lax.rem(meta[CORE] + cores - core_shift, cores)
        dp = lax.rem(meta[DP] + dps - dp_shift, dps)
        first = pl.multiple_of((core * dps + dp) * rows, rows)
        for n, (tap, col) in enumerate(targets):
            wide[m, n] = part[n].astype(F32)
            window = out.at[tap, pl.ds(first, rows), pl.ds(col, cols)]
            copy = pltpu.make_async_copy(wide.at[m, n], window, sems.at[m, n])
            copy.start()
            copies.append(copy)
    for copy in copies:
        copy.wait()


def write_taps(device, parts, shifts, groups, targets, shape, buffer, name, returned=None, after=()):
    extra, place = [] if buffer is None else [buffer], returned or []
    outs, aliases = [shape_of(shape, F32)], {}
    if place:
        outs.append(shape_of(place[1].shape, place[1].dtype))
        aliases[2 + len(parts)] = 1
    if extra:
        aliases[1 + len(parts) + len(place)] = 0
    results = call(
        functools.partial(write_taps_body, shifts, groups, targets, len(extra), len(place) // 2), device,
        (*parts, *place, *extra), [WHOLE] * len(parts) + [HBM] * (len(place) + len(extra)), outs, [HBM] * len(outs),
        scratch=[
            pltpu.VMEM((len(parts), *parts[0].shape), F32), pltpu.SemaphoreType.DMA((len(parts), len(targets))),
            *[pltpu.SemaphoreType.DMA] * (len(place) // 2),
        ],
        aliases=aliases, name=name, after=after,
    )
    return results


def act_body(meta, x, *acts):
    act = gelu(x[...].astype(F32)).astype(BF16)
    cols = acts[0].shape[1]
    for n, ref in enumerate(acts):
        ref[...] = act[:, n * cols : (n + 1) * cols]


def mm_parts(lefts, weight):
    cols = lefts[0].shape[1]
    return sum(mm(left[...], weight[0, n * cols : (n + 1) * cols]) for n, left in enumerate(lefts))


def mm_back_parts(lefts, weight):
    cols = lefts[0].shape[1]
    return sum(mm_back(left[...], weight[0, :, n * cols : (n + 1) * cols]) for n, left in enumerate(lefts))


def oth_out_body(meta, x0, x1, oth0, oth1, far0, far1, own0, own1, w_near, w_mid, w_far, out):
    cols = x0.shape[1]
    conv = mm_parts((oth0, oth1), w_mid) + mm_parts((far0, far1), w_near) + mm_parts((own0, own1), w_far)
    out[:, :cols] = (x0[...].astype(F32) + conv[:, :cols]).astype(BF16)
    out[:, cols:] = (x1[...].astype(F32) + conv[:, cols:]).astype(BF16)


def own_out_body(meta, x, own0, own1, oth0, oth1, far0, far1, w_near, w_mid, w_far, out):
    conv = mm_parts((own0, own1), w_mid) + mm_parts((oth0, oth1), w_near) + mm_parts((far0, far1), w_far)
    out[...] = (x[...].astype(F32) + conv).astype(BF16)


def outer_first_body(steps, count, meta, own0, own1, oth0, oth1, far0, far1, own_far0, own_far1, u_own, u_oth, mid, *refs):
    keep, send, rest, total = refs
    i = pl.program_id(0)

    @pl.when(i == 0)
    def _():
        total[...] = jnp.zeros_like(total)
        rest[...] = jnp.zeros_like(rest)

    cols = own0.shape[1]
    for n, (own, oth, far, own_far) in enumerate(((own0, oth0, far0, own_far0), (own1, oth1, far1, own_far1))):
        rows = slice(n * cols, (n + 1) * cols)
        u_first, u_second = u_own[:, :cols], u_own[:, cols:]
        total[0, rows] += mm_outer(own[...], u_oth[...]) + mm_outer(own_far[...], u_first)
        total[1, rows] += mm_outer(far[...], u_oth[...]) + mm_outer(oth[...], u_first)
        rest[0, rows] += mm_outer(own_far[...], u_second)
        rest[1, rows] += mm_outer(oth[...], u_second)

    @pl.when(i == steps - 1)
    def _():
        lead = 0
        for part in (mid, total):
            window = pl.ds(lead, part.shape[0])
            split_into(part, meta[CORE], count, keep.at[window], [send.at[window]])
            lead += part.shape[0]


def outer_second_body(steps, count, meta, own0, own1, far0, far1, u_oth, rest, keep, send, total):
    i = pl.program_id(0)

    @pl.when(i == 0)
    def _():
        total[...] = rest[...]

    cols = own0.shape[1]
    for n, (own, far) in enumerate(((own0, far0), (own1, far1))):
        rows = slice(n * cols, (n + 1) * cols)
        total[0, rows] += mm_outer(own[...], u_oth[...])
        total[1, rows] += mm_outer(far[...], u_oth[...])

    @pl.when(i == steps - 1)
    def _():
        split_into(total, meta[CORE], count, keep, [send])


def oth_grad_body(meta, x0, x1, u_own, oth0, oth1, far, w_near, w_mid, w_far, grad):
    cols = oth0.shape[1]
    grad_act = mm_back(u_own[...], w_near[0]) + mm_back_parts((oth0, oth1), w_mid) + mm_back(far[...], w_far[0])
    for n, (x, u) in enumerate(((x0, oth0), (x1, oth1))):
        part = slice(n * cols, (n + 1) * cols)
        _, slope = gelu_and_slope(x[...].astype(F32))
        grad[:, part] = (u[...].astype(F32) + slope * grad_act[:, part]).astype(BF16)


def own_grad_body(
    steps, meta, x, u_own, oth0, oth1, far0, far1, w_near, w_mid, w_far, returned, buffer, grad, out, sem
):
    i = pl.program_id(0)
    copy = returned_copy(meta, returned, out, sem)

    @pl.when(i == 0)
    def _():
        copy.start()

    _, slope = gelu_and_slope(x[...].astype(F32))
    u = u_own[...]
    grad_act = mm_back(u, w_mid[0]) + mm_back_parts((oth0, oth1), w_far) + mm_back_parts((far0, far1), w_near)
    grad[...] = (u.astype(F32) + slope * grad_act).astype(BF16)

    @pl.when(i == steps - 1)
    def _():
        copy.wait()


def per_device(genome, conv_weight, upstream):
    genome, upstream = genome[0], upstream[0]
    bins, chans = genome.shape
    half, cols = bins // 2, chans // 2
    block = half // 4
    steps = half // block
    count = lax.axis_size("seq")
    index = lax.axis_index("seq")
    tap = DILATION_BINS // bins
    span = 2 * tap
    dp_count, along_count = lax.axis_size("dp"), count // span
    side, along = lax.rem(index // tap, 2), index // span
    if along_count % 2 == 0:
        along = along ^ side
    def is_even(i):
        return (i // tap) % 2 == 0

    swap_pairs = [(i, i + tap if is_even(i) else i - tap) for i in range(count)]
    outer_pairs = [(i, i - span if is_even(i) else i + span) for i in range(count)]
    outer_pairs = [(i, j) for i, j in outer_pairs if 0 <= j < count]
    inner_pairs = [(j, i) for i, j in outer_pairs]

    def swap(value):
        return lax.ppermute(value, "seq", swap_pairs)

    def outward(value):
        return lax.ppermute(value, "seq", outer_pairs)

    def inward(value):
        return lax.ppermute(value, "seq", inner_pairs)

    def to_core(value, shift=1):
        return lax.ppermute(value, "seq", [(i, i - i % tap + (i % tap + shift) % tap) for i in range(count)])

    def to_dp(value, shift=1):
        return lax.ppermute(value, "dp", [(i, (i + shift) % dp_count) for i in range(dp_count)])

    flip = 1 if along_count % 2 == 0 else 0
    bits = (along_count - 1).bit_length()
    halving = along_count == 1 << bits

    def reversed_bits(value):
        return sum(((value >> n) & 1) << (bits - 1 - n) for n in range(bits)) if halving else value

    def place_along(i):
        return reversed_bits((i // span) ^ (flip * ((i // tap) % 2)))

    def device_at(i, side, position):
        return (reversed_bits(position) ^ (flip * side)) * span + side * tap + i % tap

    def to_along(value, move):
        pairs = [(i, device_at(i, (i // tap) % 2, move(place_along(i)))) for i in range(count)]
        return lax.ppermute(value, "seq", pairs)

    def to_side(value):
        pairs = [(i, device_at(i, 1 - (i // tap) % 2, place_along(i))) for i in range(count)]
        return lax.ppermute(value, "seq", pairs)

    rows_spec = pl.BlockSpec((block, chans), lambda i, s: (i, 0))
    own_spec = pl.BlockSpec((block, chans), lambda i, s: (s[SIDE] * steps + i, 0))
    w_near = pl.BlockSpec((1, chans, chans), lambda i, s: (2 - 2 * s[SIDE], 0, 0))
    w_mid = pl.BlockSpec((1, chans, chans), lambda i, s: (1, 0, 0))
    w_far = pl.BlockSpec((1, chans, chans), lambda i, s: (2 * s[SIDE], 0, 0))
    half_shape, whole_shape = shape_of((half, chans), BF16), shape_of((bins, chans), BF16)
    along = reversed_bits(along)
    along_bits = [(along >> n) & 1 for n in reversed(range(bits))]
    meta = jnp.stack([side, lax.rem(index, tap), lax.axis_index("dp"), along, *along_bits]).astype(jnp.int32)
    device = Device(meta)

    part_spec = pl.BlockSpec((block, cols), lambda i, s: (i, 0))
    weights, weight_specs = (conv_weight,) * 3, [w_near, w_mid, w_far]

    staged = halving and (chans // tap // dp_count) % (16 * along_count) == 0

    def core_stage(parts, name, after=()):
        keep, send = parts
        keep, send = reduce(device, [[keep, to_core(send)]], dp_count, DP, dtype=BF16, name=name + "_core", after=after)
        return [keep, to_dp(send)]

    def along_stage(groups, step, after=()):
        if not staged:
            return reduce(device, groups, name=f"along{step}", after=after)
        keep, send = reduce(device, groups, 2, ALONG_BITS + step, dtype=BF16, name=f"along{step}", after=after)
        return [keep, to_along(send, lambda position: position ^ (1 << (bits - 1 - step)))]

    def side_stage(groups, after=()):
        (total,) = reduce(device, groups, swap_from=2, name="last", after=after)
        if not staged:
            together = [[i + span * j for j in range(along_count)] for i in range(span)]
            total = lax.psum(total, "seq", axis_index_groups=together)
        return [total, to_side(total)]

    def round_slice(parts, after=()):
        return reduce(device, [parts], dtype=BF16, name="side", after=after)[0]

    def spread(value):
        moves = [lambda position, s=s: (position + s) % along_count for s in range(1, along_count)]
        return [value] + [to_along(value, move) for move in moves if staged]

    def join(pieces, name, after=()):
        total = gather(device, pieces, ALONG, name, after) if staged else pieces[0]
        return [total] + [to_core(total, s) for s in range(1, tap)]

    targets = [(1, 0), (1, cols), (0, 0), (2, 0), (0, cols), (2, cols)]

    def write(joined, dp_shift, buffer, returned=None, after=()):
        shifts = [(core_shift, dp_shift) for core_shift in range(tap)]
        return write_taps(
            device, joined, shifts, (tap, dp_count), targets, conv_weight.shape, buffer, f"write_taps{dp_shift}",
            returned, after,
        )

    def slices_of(parts, dtype):
        piece = (parts, chans // tap, cols)
        return [shape_of(piece, F32), shape_of(piece, dtype)], [pl.BlockSpec(piece, lambda i, s: (0, 0, 0))] * 2

    sums_shape = (2, chans, cols)
    sums_spec = pl.BlockSpec(sums_shape, lambda i, s: (0, 0, 0))

    def oth_act(x, name, after=()):
        return call(
            act_body, device, (x,), [part_spec], shape_of((half, cols), BF16), part_spec, grid=(steps,), name=name,
            after=after,
        )

    (x_send0,) = cut(device, (genome,), [(0, False, 0, half, cols)], "cut_first")
    x_oth0 = swap(x_send0)
    a_own = call(
        act_body, device, (genome,), [own_spec], [shape_of((half, cols), BF16)] * 2, [part_spec] * 2, grid=(steps,),
        name="own_act",
    )
    a_oth_far = [outward(part) for part in a_own]
    x_send1, u_send0, u_send1, u_own = cut(
        device, (genome, upstream),
        [(0, False, cols, half, cols), (1, False, 0, half, cols), (1, False, cols, half, cols), (1, True, 0, half, chans)],
        "cut_rest",
    )
    x_oth1, u_oth = swap(x_send1), [swap(u_send0), swap(u_send1)]
    u_oth_far, u_own_far = outward(u_own), [inward(part) for part in u_oth]
    mid = call(
        lambda meta, *refs: mid_body(*refs), device, (genome, upstream), [rows_spec] * 2, shape_of(sums_shape, F32),
        sums_spec, grid=(2 * steps,), name="mid_tap",
    )
    a_oth0 = oth_act(x_oth0, "oth_act0")
    a_own_far0 = inward(a_oth0)
    a_oth1 = oth_act(x_oth1, "oth_act1")
    a_own_far1 = inward(a_oth1)
    out = call(
        oth_out_body, device, (x_oth0, x_oth1, a_oth0, a_oth1, *a_oth_far, *a_own, *weights),
        [*[part_spec] * 8, *weight_specs], half_shape, rows_spec, grid=(steps,), name="oth_out", after=(a_own_far0,),
    )
    out = swap(out)
    slices, specs = slices_of(4, BF16)
    *outer0, rest = call(
        functools.partial(outer_first_body, steps, tap), device,
        (*a_own, a_oth0, a_oth1, *a_oth_far, a_own_far0, a_own_far1, u_own, u_oth[0], mid),
        [*[part_spec] * 8, rows_spec, part_spec, WHOLE], [*slices, shape_of(sums_shape, F32)], [*specs, sums_spec],
        grid=(steps,), scratch=[pltpu.VMEM(sums_shape, F32)], name="outer_first",
    )
    slices, specs = slices_of(2, F32)
    outer1 = call(
        functools.partial(outer_second_body, steps, tap), device, (*a_own, *a_oth_far, u_oth[1], rest),
        [*[part_spec] * 5, WHOLE], slices, specs, grid=(steps,), scratch=[pltpu.VMEM(sums_shape, F32)],
        name="outer_second",
    )
    outer0 = core_stage(outer0, "outer0", after=(u_own_far[0],))
    outer1 = core_stage(outer1, "outer1")
    grad = call(
        oth_grad_body, device, (x_oth0, x_oth1, u_own, *u_oth, u_oth_far, *weights),
        [part_spec, part_spec, rows_spec, part_spec, part_spec, rows_spec, *weight_specs], half_shape, rows_spec,
        grid=(steps,), name="oth_grad",
    )
    grad = swap(grad)
    parts = along_stage([outer0, outer1], 0)
    output = call(
        own_out_body, device, (genome, *a_own, a_oth0, a_oth1, a_own_far0, a_own_far1, *weights),
        [own_spec, *[part_spec] * 6, *weight_specs], whole_shape, own_spec, grid=(steps,), name="own_out",
    )
    parts = along_stage([parts], 1)
    grad_genome, output = call(
        functools.partial(own_grad_body, steps), device,
        (genome, u_own, *u_oth, *u_own_far, *weights, out, output),
        [own_spec, rows_spec, *[part_spec] * 4, *weight_specs, HBM, HBM], [whole_shape] * 2, [own_spec, HBM],
        grid=(steps,), scratch=[pltpu.SemaphoreType.DMA], aliases={11: 1}, name="own_grad",
    )
    parts = side_stage([parts])
    last_slice = round_slice(parts)
    far_slices = [to_dp(last_slice, s) for s in range(1, dp_count)]
    pieces = spread(last_slice)
    far_pieces = [[far] + [to_dp(piece, s) for piece in pieces[1:]] for s, far in enumerate(far_slices, 1)]
    joined = join(pieces, "join")
    joined_far = [join(far, f"join_far{s}") for s, far in enumerate(far_pieces, 1)]
    grad_weight, grad_genome = write(joined, 0, None, [grad, grad_genome])
    for s, far in enumerate(joined_far, 1):
        (grad_weight,) = write(far, s, grad_weight)
    return (output[None], grad_genome[None], grad_weight)


def solution(mesh):
    return jax.shard_map(
        per_device,
        mesh=mesh,
        in_specs=(P("dp", "seq", None), P(), P("dp", "seq", None)),
        out_specs=(P("dp", "seq", None), P("dp", "seq", None), P()),
        check_vma=False,
    )
```

```python
import functools

import jax
import jax.numpy as jnp
from jax import lax
from jax.experimental import pallas as pl
from jax.experimental.pallas import tpu as pltpu
from jax.sharding import PartitionSpec as P

DILATION_BINS = 4096
BF16, F32 = jnp.bfloat16, jnp.float32
VMEM_BYTES = 40 * 1024 * 1024
SIDE, CORE, DP, ALONG, ALONG_BITS = range(5)
HBM = pl.BlockSpec(memory_space=pltpu.HBM)
WHOLE = pl.BlockSpec(memory_space=pltpu.VMEM)


def shape_of(shape, dtype):
    return jax.ShapeDtypeStruct(shape, dtype)


TOKEN = jax.ShapeDtypeStruct((8, 128), F32)


class Device:
    def __init__(self, meta):
        self.meta, self.token = meta, None


def call(
    body, device, operands, in_specs, outs, out_specs, grid=(), scratch=(), aliases=None, name=None, after=()
):
    first = device.token is None
    n_in, single = len(operands), not isinstance(outs, list)
    outs, out_specs = ([outs], [out_specs]) if single else (outs, out_specs)
    n_out = len(outs)
    tokens = [*after] if first else [device.token, *after]

    def chained(meta, *refs):
        rest = refs[n_in + len(tokens) :]
        body(meta, *refs[:n_in], *rest[:n_out], *rest[n_out + 1 :])

    results = pl.pallas_call(
        chained,
        grid_spec=pltpu.PrefetchScalarGridSpec(
            num_scalar_prefetch=1, grid=grid, in_specs=[*in_specs, *[HBM] * len(tokens)], out_specs=[*out_specs, HBM],
            scratch_shapes=list(scratch),
        ),
        out_shape=[*outs, TOKEN],
        input_output_aliases=aliases or {},
        compiler_params=pltpu.CompilerParams(vmem_limit_bytes=VMEM_BYTES),
        cost_estimate=pl.CostEstimate(flops=1, bytes_accessed=200_000, transcendentals=0),
        name=name,
    )(device.meta, *operands, *tokens)
    device.token = results[-1]
    return results[0] if single else results[:-1]


def gelu_parts(x):
    k = 0.7978845608028654
    square = x * x
    t = jnp.tanh(k * (x * (1.0 + 0.044715 * square)))
    return t, square, k


def gelu(x):
    t, _, _ = gelu_parts(x)
    return x * (0.5 * (1.0 + t))


def gelu_and_slope(x):
    t, square, k = gelu_parts(x)
    cdf = 0.5 * (1.0 + t)
    slope = cdf + 0.5 * x * (1.0 - t * t) * (k + (3 * 0.044715 * k) * square)
    return x * cdf, slope


def mm(left, right):
    return lax.dot_general(left, right, (((1,), (0,)), ((), ())), preferred_element_type=F32)


def mm_back(left, right):
    return lax.dot_general(left, right, (((1,), (1,)), ((), ())), preferred_element_type=F32)


def mm_outer(left, right):
    return lax.dot_general(left, right, (((0,), (0,)), ((), ())), preferred_element_type=F32)


def cut_body(plan, n_in, meta, *refs):
    ins, outs, sems = refs[:n_in], refs[n_in:-1], refs[-1]
    copies = []
    for n, (which, own, col, rows, cols) in enumerate(plan):
        start = (meta[SIDE] if own else 1 - meta[SIDE]) * rows
        window = ins[which].at[pl.ds(pl.multiple_of(start, rows), rows), pl.ds(col, cols)]
        copies.append(pltpu.make_async_copy(window, outs[n], sems.at[n]))
    for copy in copies:
        copy.start()
    for copy in copies:
        copy.wait()


def cut(device, operands, plan, name):
    outs = [shape_of((rows, cols), BF16) for _, _, _, rows, cols in plan]
    return call(
        functools.partial(cut_body, plan, len(operands)), device, operands, [HBM] * len(operands), outs,
        [HBM] * len(plan), scratch=[pltpu.SemaphoreType.DMA((len(plan),))], name=name,
    )


def split_into(total, position, count, keep, sends):
    size = total.shape[1] // count
    for shift, ref in enumerate((keep, *sends)):
        there = lax.rem(position + shift, count)
        ref[...] = total[:, pl.ds(pl.multiple_of(there * size, size), size), :].astype(ref.dtype)


def mid_body(x, u, total):
    @pl.when(pl.program_id(0) == 0)
    def _():
        total[...] = jnp.zeros_like(total)

    cols = total.shape[2]
    product = mm_outer(gelu(x[...].astype(F32)).astype(BF16), u[...])
    for part in range(2):
        total[part] += product[:, part * cols : (part + 1) * cols]


def reduce_body(sizes, n_out, place, swap_from, meta, *refs):
    ins, outs, total = refs[: sum(sizes)], refs[sum(sizes) : -1], refs[-1]
    first = lead = 0
    for size in sizes:
        value = ins[first][...].astype(F32)
        for ref in ins[first + 1 : first + size]:
            value = value + ref[...].astype(F32)
        total[lead : lead + value.shape[0]] = value
        first, lead = first + size, lead + value.shape[0]
    for part in range(swap_from, lead, 2):
        pair = total[part : part + 2]
        for n in range(2):
            total[part + n] = jnp.where(meta[SIDE] == 0, pair[n], pair[1 - n])
    if n_out > 1:
        split_into(total, meta[place], n_out, outs[0], outs[1:])
    else:
        outs[0][...] = total[...].astype(outs[0].dtype)


def reduce(device, groups, n_out=1, place=None, swap_from=None, dtype=F32, name=None, after=()):
    _, rows, cols = groups[0][0].shape
    k = sum(group[0].shape[0] for group in groups)
    values = [value for group in groups for value in group]
    dtypes = [dtype] if n_out == 1 else [F32] + [dtype] * (n_out - 1)
    outs = [shape_of((k, rows // n_out, cols), each) for each in dtypes]
    sizes = [len(group) for group in groups]
    body = functools.partial(reduce_body, sizes, n_out, place, k if swap_from is None else swap_from)
    return call(
        body, device, values, [WHOLE] * len(values), outs, [WHOLE] * n_out,
        scratch=[pltpu.VMEM((k, rows, cols), F32)], name=name, after=after,
    )


def gather_body(count, place, meta, *refs):
    ins, out = refs[:count], refs[count]
    size = ins[0].shape[1]
    for shift, ref in enumerate(ins):
        source = lax.rem(meta[place] + count - shift, count)
        out[:, pl.ds(pl.multiple_of(source * size, size), size), :] = ref[...]


def gather(device, values, place, name=None, after=()):
    count = len(values)
    k, rows, cols = values[0].shape
    return call(
        functools.partial(gather_body, count, place), device, values, [WHOLE] * count,
        shape_of((k, rows * count, cols), BF16), WHOLE, name=name, after=after,
    )


def returned_copy(meta, part, out, sem):
    rows = part.shape[0]
    start = pl.multiple_of((1 - meta[SIDE]) * rows, rows)
    return pltpu.make_async_copy(part, out.at[pl.ds(start, rows)], sem)


def write_taps_body(shifts, groups, targets, aliased, placing, meta, *refs):
    parts, refs = refs[: len(shifts)], refs[len(shifts) :]
    returned, refs = refs[: 2 * placing], refs[2 * placing + aliased :]
    out, wide, sems = refs[0], refs[-2 - placing], refs[-1 - placing]
    rows, cols = parts[0].shape[1:]
    cores, dps = groups
    copies = []
    if placing:
        copies.append(returned_copy(meta, returned[0], refs[1], refs[-1]))
        copies[0].start()
    for m, (part, (core_shift, dp_shift)) in enumerate(zip(parts, shifts)):
        core = lax.rem(meta[CORE] + cores - core_shift, cores)
        dp = lax.rem(meta[DP] + dps - dp_shift, dps)
        first = pl.multiple_of((core * dps + dp) * rows, rows)
        for n, (tap, col) in enumerate(targets):
            wide[m, n] = part[n].astype(F32)
            window = out.at[tap, pl.ds(first, rows), pl.ds(col, cols)]
            copy = pltpu.make_async_copy(wide.at[m, n], window, sems.at[m, n])
            copy.start()
            copies.append(copy)
    for copy in copies:
        copy.wait()


def write_taps(device, parts, shifts, groups, targets, shape, buffer, name, returned=None, after=()):
    extra, place = [] if buffer is None else [buffer], returned or []
    outs, aliases = [shape_of(shape, F32)], {}
    if place:
        outs.append(shape_of(place[1].shape, place[1].dtype))
        aliases[2 + len(parts)] = 1
    if extra:
        aliases[1 + len(parts) + len(place)] = 0
    results = call(
        functools.partial(write_taps_body, shifts, groups, targets, len(extra), len(place) // 2), device,
        (*parts, *place, *extra), [WHOLE] * len(parts) + [HBM] * (len(place) + len(extra)), outs, [HBM] * len(outs),
        scratch=[
            pltpu.VMEM((len(parts), *parts[0].shape), F32), pltpu.SemaphoreType.DMA((len(parts), len(targets))),
            *[pltpu.SemaphoreType.DMA] * (len(place) // 2),
        ],
        aliases=aliases, name=name, after=after,
    )
    return results


def act_body(meta, x, *acts):
    act = gelu(x[...].astype(F32)).astype(BF16)
    cols = acts[0].shape[1]
    for n, ref in enumerate(acts):
        ref[...] = act[:, n * cols : (n + 1) * cols]


def mm_parts(lefts, weight):
    cols = lefts[0].shape[1]
    return sum(mm(left[...], weight[0, n * cols : (n + 1) * cols]) for n, left in enumerate(lefts))


def mm_back_parts(lefts, weight):
    cols = lefts[0].shape[1]
    return sum(mm_back(left[...], weight[0, :, n * cols : (n + 1) * cols]) for n, left in enumerate(lefts))


def oth_out_body(meta, x0, x1, oth0, oth1, far0, far1, own0, own1, w_near, w_mid, w_far, out):
    cols = x0.shape[1]
    conv = mm_parts((oth0, oth1), w_mid) + mm_parts((far0, far1), w_near) + mm_parts((own0, own1), w_far)
    out[:, :cols] = (x0[...].astype(F32) + conv[:, :cols]).astype(BF16)
    out[:, cols:] = (x1[...].astype(F32) + conv[:, cols:]).astype(BF16)


def own_out_body(meta, x, own0, own1, oth0, oth1, far0, far1, w_near, w_mid, w_far, out):
    conv = mm_parts((own0, own1), w_mid) + mm_parts((oth0, oth1), w_near) + mm_parts((far0, far1), w_far)
    out[...] = (x[...].astype(F32) + conv).astype(BF16)


def outer_first_body(steps, count, meta, own0, own1, oth0, oth1, far0, far1, own_far0, own_far1, u_own, u_oth, mid, *refs):
    keep, send, rest, total = refs
    i = pl.program_id(0)

    @pl.when(i == 0)
    def _():
        total[...] = jnp.zeros_like(total)
        rest[...] = jnp.zeros_like(rest)

    cols = own0.shape[1]
    for n, (own, oth, far, own_far) in enumerate(((own0, oth0, far0, own_far0), (own1, oth1, far1, own_far1))):
        rows = slice(n * cols, (n + 1) * cols)
        u_first, u_second = u_own[:, :cols], u_own[:, cols:]
        total[0, rows] += mm_outer(own[...], u_oth[...]) + mm_outer(own_far[...], u_first)
        total[1, rows] += mm_outer(far[...], u_oth[...]) + mm_outer(oth[...], u_first)
        rest[0, rows] += mm_outer(own_far[...], u_second)
        rest[1, rows] += mm_outer(oth[...], u_second)

    @pl.when(i == steps - 1)
    def _():
        lead = 0
        for part in (mid, total):
            window = pl.ds(lead, part.shape[0])
            split_into(part, meta[CORE], count, keep.at[window], [send.at[window]])
            lead += part.shape[0]


def outer_second_body(steps, count, meta, own0, own1, far0, far1, u_oth, rest, keep, send, total):
    i = pl.program_id(0)

    @pl.when(i == 0)
    def _():
        total[...] = rest[...]

    cols = own0.shape[1]
    for n, (own, far) in enumerate(((own0, far0), (own1, far1))):
        rows = slice(n * cols, (n + 1) * cols)
        total[0, rows] += mm_outer(own[...], u_oth[...])
        total[1, rows] += mm_outer(far[...], u_oth[...])

    @pl.when(i == steps - 1)
    def _():
        split_into(total, meta[CORE], count, keep, [send])


def oth_grad_body(meta, x0, x1, u_own, oth0, oth1, far, w_near, w_mid, w_far, grad):
    cols = oth0.shape[1]
    grad_act = mm_back(u_own[...], w_near[0]) + mm_back_parts((oth0, oth1), w_mid) + mm_back(far[...], w_far[0])
    for n, (x, u) in enumerate(((x0, oth0), (x1, oth1))):
        part = slice(n * cols, (n + 1) * cols)
        _, slope = gelu_and_slope(x[...].astype(F32))
        grad[:, part] = (u[...].astype(F32) + slope * grad_act[:, part]).astype(BF16)


def own_grad_body(
    steps, meta, x, u_own, oth0, oth1, far0, far1, w_near, w_mid, w_far, returned, buffer, grad, out, sem
):
    i = pl.program_id(0)
    copy = returned_copy(meta, returned, out, sem)

    @pl.when(i == 0)
    def _():
        copy.start()

    _, slope = gelu_and_slope(x[...].astype(F32))
    u = u_own[...]
    grad_act = mm_back(u, w_mid[0]) + mm_back_parts((oth0, oth1), w_far) + mm_back_parts((far0, far1), w_near)
    grad[...] = (u.astype(F32) + slope * grad_act).astype(BF16)

    @pl.when(i == steps - 1)
    def _():
        copy.wait()


def per_device(genome, conv_weight, upstream):
    genome, upstream = genome[0], upstream[0]
    bins, chans = genome.shape
    half, cols = bins // 2, chans // 2
    block = half // 4
    steps = half // block
    count = lax.axis_size("seq")
    index = lax.axis_index("seq")
    tap = DILATION_BINS // bins
    span = 2 * tap
    dp_count, along_count = lax.axis_size("dp"), count // span
    side, along = lax.rem(index // tap, 2), index // span
    if along_count % 2 == 0:
        along = along ^ side
    def is_even(i):
        return (i // tap) % 2 == 0

    swap_pairs = [(i, i + tap if is_even(i) else i - tap) for i in range(count)]
    outer_pairs = [(i, i - span if is_even(i) else i + span) for i in range(count)]
    outer_pairs = [(i, j) for i, j in outer_pairs if 0 <= j < count]
    inner_pairs = [(j, i) for i, j in outer_pairs]

    def swap(value):
        return lax.ppermute(value, "seq", swap_pairs)

    def outward(value):
        return lax.ppermute(value, "seq", outer_pairs)

    def inward(value):
        return lax.ppermute(value, "seq", inner_pairs)

    def to_core(value, shift=1):
        return lax.ppermute(value, "seq", [(i, i - i % tap + (i % tap + shift) % tap) for i in range(count)])

    def to_dp(value, shift=1):
        return lax.ppermute(value, "dp", [(i, (i + shift) % dp_count) for i in range(dp_count)])

    flip = 1 if along_count % 2 == 0 else 0
    bits = (along_count - 1).bit_length()
    halving = along_count == 1 << bits

    def reversed_bits(value):
        return sum(((value >> n) & 1) << (bits - 1 - n) for n in range(bits)) if halving else value

    def place_along(i):
        return reversed_bits((i // span) ^ (flip * ((i // tap) % 2)))

    def device_at(i, side, position):
        return (reversed_bits(position) ^ (flip * side)) * span + side * tap + i % tap

    def to_along(value, move):
        pairs = [(i, device_at(i, (i // tap) % 2, move(place_along(i)))) for i in range(count)]
        return lax.ppermute(value, "seq", pairs)

    def to_side(value):
        pairs = [(i, device_at(i, 1 - (i // tap) % 2, place_along(i))) for i in range(count)]
        return lax.ppermute(value, "seq", pairs)

    rows_spec = pl.BlockSpec((block, chans), lambda i, s: (i, 0))
    own_spec = pl.BlockSpec((block, chans), lambda i, s: (s[SIDE] * steps + i, 0))
    w_near = pl.BlockSpec((1, chans, chans), lambda i, s: (2 - 2 * s[SIDE], 0, 0))
    w_mid = pl.BlockSpec((1, chans, chans), lambda i, s: (1, 0, 0))
    w_far = pl.BlockSpec((1, chans, chans), lambda i, s: (2 * s[SIDE], 0, 0))
    half_shape, whole_shape = shape_of((half, chans), BF16), shape_of((bins, chans), BF16)
    along = reversed_bits(along)
    along_bits = [(along >> n) & 1 for n in reversed(range(bits))]
    meta = jnp.stack([side, lax.rem(index, tap), lax.axis_index("dp"), along, *along_bits]).astype(jnp.int32)
    device = Device(meta)

    part_spec = pl.BlockSpec((block, cols), lambda i, s: (i, 0))
    part_wide = pl.BlockSpec((2 * block, cols), lambda i, s: (i, 0))
    rows_wide = pl.BlockSpec((2 * block, chans), lambda i, s: (i, 0))
    weights, weight_specs = (conv_weight,) * 3, [w_near, w_mid, w_far]

    staged = halving and (chans // tap // dp_count) % (16 * along_count) == 0

    def core_stage(parts, name, after=()):
        keep, send = parts
        keep, send = reduce(device, [[keep, to_core(send)]], dp_count, DP, dtype=BF16, name=name + "_core", after=after)
        return [keep, to_dp(send)]

    def along_stage(groups, step, after=()):
        if not staged:
            return reduce(device, groups, name=f"along{step}", after=after)
        keep, send = reduce(device, groups, 2, ALONG_BITS + step, dtype=BF16, name=f"along{step}", after=after)
        return [keep, to_along(send, lambda position: position ^ (1 << (bits - 1 - step)))]

    def side_stage(groups, after=()):
        (total,) = reduce(device, groups, swap_from=2, name="last", after=after)
        if not staged:
            together = [[i + span * j for j in range(along_count)] for i in range(span)]
            total = lax.psum(total, "seq", axis_index_groups=together)
        return [total, to_side(total)]

    def round_slice(parts, after=()):
        return reduce(device, [parts], dtype=BF16, name="side", after=after)[0]

    def spread(value):
        moves = [lambda position, s=s: (position + s) % along_count for s in range(1, along_count)]
        return [value] + [to_along(value, move) for move in moves if staged]

    def join(pieces, name, after=()):
        total = gather(device, pieces, ALONG, name, after) if staged else pieces[0]
        return [total] + [to_core(total, s) for s in range(1, tap)]

    targets = [(1, 0), (1, cols), (0, 0), (2, 0), (0, cols), (2, cols)]

    def write(joined, dp_shift, buffer, returned=None, after=()):
        shifts = [(core_shift, dp_shift) for core_shift in range(tap)]
        return write_taps(
            device, joined, shifts, (tap, dp_count), targets, conv_weight.shape, buffer, f"write_taps{dp_shift}",
            returned, after,
        )

    def slices_of(parts, dtype):
        piece = (parts, chans // tap, cols)
        return [shape_of(piece, F32), shape_of(piece, dtype)], [pl.BlockSpec(piece, lambda i, s: (0, 0, 0))] * 2

    sums_shape = (2, chans, cols)
    sums_spec = pl.BlockSpec(sums_shape, lambda i, s: (0, 0, 0))

    def oth_act(x, name, after=()):
        return call(
            act_body, device, (x,), [part_spec], shape_of((half, cols), BF16), part_spec, grid=(steps,), name=name,
            after=after,
        )

    (x_send0,) = cut(device, (genome,), [(0, False, 0, half, cols)], "cut_first")
    x_oth0 = swap(x_send0)
    a_own = call(
        act_body, device, (genome,), [own_spec], [shape_of((half, cols), BF16)] * 2, [part_spec] * 2, grid=(steps,),
        name="own_act",
    )
    a_oth_far = [outward(part) for part in a_own]
    x_send1, u_send0, u_send1, u_own = cut(
        device, (genome, upstream),
        [(0, False, cols, half, cols), (1, False, 0, half, cols), (1, False, cols, half, cols), (1, True, 0, half, chans)],
        "cut_rest",
    )
    x_oth1, u_oth = swap(x_send1), [swap(u_send0), swap(u_send1)]
    u_oth_far, u_own_far = outward(u_own), [inward(part) for part in u_oth]
    mid = call(
        lambda meta, *refs: mid_body(*refs), device, (genome, upstream), [rows_spec] * 2, shape_of(sums_shape, F32),
        sums_spec, grid=(2 * steps,), name="mid_tap",
    )
    a_oth0 = oth_act(x_oth0, "oth_act0")
    a_own_far0 = inward(a_oth0)
    a_oth1 = oth_act(x_oth1, "oth_act1")
    a_own_far1 = inward(a_oth1)
    out = call(
        oth_out_body, device, (x_oth0, x_oth1, a_oth0, a_oth1, *a_oth_far, *a_own, *weights),
        [*[part_spec] * 8, *weight_specs], half_shape, rows_spec, grid=(steps,), name="oth_out", after=(a_own_far0,),
    )
    out = swap(out)
    slices, specs = slices_of(4, BF16)
    *outer0, rest = call(
        functools.partial(outer_first_body, steps // 2, tap), device,
        (*a_own, a_oth0, a_oth1, *a_oth_far, a_own_far0, a_own_far1, u_own, u_oth[0], mid),
        [*[part_wide] * 8, rows_wide, part_wide, WHOLE], [*slices, shape_of(sums_shape, F32)], [*specs, sums_spec],
        grid=(steps // 2,), scratch=[pltpu.VMEM(sums_shape, F32)], name="outer_first",
    )
    slices, specs = slices_of(2, F32)
    outer1 = call(
        functools.partial(outer_second_body, steps // 2, tap), device, (*a_own, *a_oth_far, u_oth[1], rest),
        [*[part_wide] * 5, WHOLE], slices, specs, grid=(steps // 2,), scratch=[pltpu.VMEM(sums_shape, F32)],
        name="outer_second",
    )
    outer0 = core_stage(outer0, "outer0", after=(u_own_far[0],))
    outer1 = core_stage(outer1, "outer1")
    grad = call(
        oth_grad_body, device, (x_oth0, x_oth1, u_own, *u_oth, u_oth_far, *weights),
        [part_spec, part_spec, rows_spec, part_spec, part_spec, rows_spec, *weight_specs], half_shape, rows_spec,
        grid=(steps,), name="oth_grad",
    )
    grad = swap(grad)
    parts = along_stage([outer0, outer1], 0)
    output = call(
        own_out_body, device, (genome, *a_own, a_oth0, a_oth1, a_own_far0, a_own_far1, *weights),
        [own_spec, *[part_spec] * 6, *weight_specs], whole_shape, own_spec, grid=(steps,), name="own_out",
    )
    parts = along_stage([parts], 1)
    grad_genome, output = call(
        functools.partial(own_grad_body, steps), device,
        (genome, u_own, *u_oth, *u_own_far, *weights, out, output),
        [own_spec, rows_spec, *[part_spec] * 4, *weight_specs, HBM, HBM], [whole_shape] * 2, [own_spec, HBM],
        grid=(steps,), scratch=[pltpu.SemaphoreType.DMA], aliases={11: 1}, name="own_grad",
    )
    parts = side_stage([parts])
    last_slice = round_slice(parts)
    far_slices = [to_dp(last_slice, s) for s in range(1, dp_count)]
    pieces = spread(last_slice)
    far_pieces = [[far] + [to_dp(piece, s) for piece in pieces[1:]] for s, far in enumerate(far_slices, 1)]
    joined = join(pieces, "join")
    joined_far = [join(far, f"join_far{s}") for s, far in enumerate(far_pieces, 1)]
    grad_weight, grad_genome = write(joined, 0, None, [grad, grad_genome])
    for s, far in enumerate(joined_far, 1):
        (grad_weight,) = write(far, s, grad_weight)
    return (output[None], grad_genome[None], grad_weight)


def solution(mesh):
    return jax.shard_map(
        per_device,
        mesh=mesh,
        in_specs=(P("dp", "seq", None), P(), P("dp", "seq", None)),
        out_specs=(P("dp", "seq", None), P("dp", "seq", None), P()),
        check_vma=False,
    )
```

```python
import functools

import jax
import jax.numpy as jnp
from jax import lax
from jax.experimental import pallas as pl
from jax.experimental.pallas import tpu as pltpu
from jax.sharding import PartitionSpec as P

DILATION_BINS = 4096
BF16, F32 = jnp.bfloat16, jnp.float32
VMEM_BYTES = 40 * 1024 * 1024
SIDE, CORE, DP, ALONG, ALONG_BITS = range(5)
HBM = pl.BlockSpec(memory_space=pltpu.HBM)
WHOLE = pl.BlockSpec(memory_space=pltpu.VMEM)


def shape_of(shape, dtype):
    return jax.ShapeDtypeStruct(shape, dtype)


TOKEN = jax.ShapeDtypeStruct((8, 128), F32)


class Device:
    def __init__(self, meta):
        self.meta, self.token = meta, None


def call(
    body, device, operands, in_specs, outs, out_specs, grid=(), scratch=(), aliases=None, name=None, after=()
):
    first = device.token is None
    n_in, single = len(operands), not isinstance(outs, list)
    outs, out_specs = ([outs], [out_specs]) if single else (outs, out_specs)
    n_out = len(outs)
    tokens = [*after] if first else [device.token, *after]

    def chained(meta, *refs):
        rest = refs[n_in + len(tokens) :]
        body(meta, *refs[:n_in], *rest[:n_out], *rest[n_out + 1 :])

    results = pl.pallas_call(
        chained,
        grid_spec=pltpu.PrefetchScalarGridSpec(
            num_scalar_prefetch=1, grid=grid, in_specs=[*in_specs, *[HBM] * len(tokens)], out_specs=[*out_specs, HBM],
            scratch_shapes=list(scratch),
        ),
        out_shape=[*outs, TOKEN],
        input_output_aliases=aliases or {},
        compiler_params=pltpu.CompilerParams(vmem_limit_bytes=VMEM_BYTES),
        cost_estimate=pl.CostEstimate(flops=1, bytes_accessed=200_000, transcendentals=0),
        name=name,
    )(device.meta, *operands, *tokens)
    device.token = results[-1]
    return results[0] if single else results[:-1]


def gelu_parts(x):
    k = 0.7978845608028654
    square = x * x
    t = jnp.tanh(k * (x * (1.0 + 0.044715 * square)))
    return t, square, k


def gelu(x):
    t, _, _ = gelu_parts(x)
    return x * (0.5 * (1.0 + t))


def gelu_and_slope(x):
    t, square, k = gelu_parts(x)
    cdf = 0.5 * (1.0 + t)
    slope = cdf + 0.5 * x * (1.0 - t * t) * (k + (3 * 0.044715 * k) * square)
    return x * cdf, slope


def mm(left, right):
    return lax.dot_general(left, right, (((1,), (0,)), ((), ())), preferred_element_type=F32)


def mm_back(left, right):
    return lax.dot_general(left, right, (((1,), (1,)), ((), ())), preferred_element_type=F32)


def mm_outer(left, right):
    return lax.dot_general(left, right, (((0,), (0,)), ((), ())), preferred_element_type=F32)


def cut_body(plan, n_in, meta, *refs):
    ins, outs, sems = refs[:n_in], refs[n_in:-1], refs[-1]
    copies = []
    for n, (which, own, col, rows, cols) in enumerate(plan):
        start = (meta[SIDE] if own else 1 - meta[SIDE]) * rows
        window = ins[which].at[pl.ds(pl.multiple_of(start, rows), rows), pl.ds(col, cols)]
        copies.append(pltpu.make_async_copy(window, outs[n], sems.at[n]))
    for copy in copies:
        copy.start()
    for copy in copies:
        copy.wait()


def cut(device, operands, plan, name):
    outs = [shape_of((rows, cols), BF16) for _, _, _, rows, cols in plan]
    return call(
        functools.partial(cut_body, plan, len(operands)), device, operands, [HBM] * len(operands), outs,
        [HBM] * len(plan), scratch=[pltpu.SemaphoreType.DMA((len(plan),))], name=name,
    )


def split_into(total, position, count, keep, sends):
    size = total.shape[1] // count
    for shift, ref in enumerate((keep, *sends)):
        there = lax.rem(position + shift, count)
        ref[...] = total[:, pl.ds(pl.multiple_of(there * size, size), size), :].astype(ref.dtype)


def mid_body(x, u, total):
    @pl.when(pl.program_id(0) == 0)
    def _():
        total[...] = jnp.zeros_like(total)

    cols = total.shape[2]
    product = mm_outer(gelu(x[...].astype(F32)).astype(BF16), u[...])
    for part in range(2):
        total[part] += product[:, part * cols : (part + 1) * cols]


def reduce_body(sizes, n_out, place, swap_from, meta, *refs):
    ins, outs, total = refs[: sum(sizes)], refs[sum(sizes) : -1], refs[-1]
    first = lead = 0
    for size in sizes:
        value = ins[first][...].astype(F32)
        for ref in ins[first + 1 : first + size]:
            value = value + ref[...].astype(F32)
        total[lead : lead + value.shape[0]] = value
        first, lead = first + size, lead + value.shape[0]
    for part in range(swap_from, lead, 2):
        pair = total[part : part + 2]
        for n in range(2):
            total[part + n] = jnp.where(meta[SIDE] == 0, pair[n], pair[1 - n])
    if n_out > 1:
        split_into(total, meta[place], n_out, outs[0], outs[1:])
    else:
        outs[0][...] = total[...].astype(outs[0].dtype)


def reduce(device, groups, n_out=1, place=None, swap_from=None, dtype=F32, name=None, after=()):
    _, rows, cols = groups[0][0].shape
    k = sum(group[0].shape[0] for group in groups)
    values = [value for group in groups for value in group]
    dtypes = [dtype] if n_out == 1 else [F32] + [dtype] * (n_out - 1)
    outs = [shape_of((k, rows // n_out, cols), each) for each in dtypes]
    sizes = [len(group) for group in groups]
    body = functools.partial(reduce_body, sizes, n_out, place, k if swap_from is None else swap_from)
    return call(
        body, device, values, [WHOLE] * len(values), outs, [WHOLE] * n_out,
        scratch=[pltpu.VMEM((k, rows, cols), F32)], name=name, after=after,
    )


def gather_body(count, place, meta, *refs):
    ins, out = refs[:count], refs[count]
    size = ins[0].shape[1]
    for shift, ref in enumerate(ins):
        source = lax.rem(meta[place] + count - shift, count)
        out[:, pl.ds(pl.multiple_of(source * size, size), size), :] = ref[...]


def gather(device, values, place, name=None, after=()):
    count = len(values)
    k, rows, cols = values[0].shape
    return call(
        functools.partial(gather_body, count, place), device, values, [WHOLE] * count,
        shape_of((k, rows * count, cols), BF16), WHOLE, name=name, after=after,
    )


def returned_copy(meta, part, out, sem):
    rows = part.shape[0]
    start = pl.multiple_of((1 - meta[SIDE]) * rows, rows)
    return pltpu.make_async_copy(part, out.at[pl.ds(start, rows)], sem)


def write_taps_body(shifts, groups, targets, aliased, placing, meta, *refs):
    parts, refs = refs[: len(shifts)], refs[len(shifts) :]
    returned, refs = refs[: 2 * placing], refs[2 * placing + aliased :]
    out, wide, sems = refs[0], refs[-2 - placing], refs[-1 - placing]
    rows, cols = parts[0].shape[1:]
    cores, dps = groups
    copies = []
    if placing:
        copies.append(returned_copy(meta, returned[0], refs[1], refs[-1]))
        copies[0].start()
    for m, (part, (core_shift, dp_shift)) in enumerate(zip(parts, shifts)):
        core = lax.rem(meta[CORE] + cores - core_shift, cores)
        dp = lax.rem(meta[DP] + dps - dp_shift, dps)
        first = pl.multiple_of((core * dps + dp) * rows, rows)
        for n, (tap, col) in enumerate(targets):
            wide[m, n] = part[n].astype(F32)
            window = out.at[tap, pl.ds(first, rows), pl.ds(col, cols)]
            copy = pltpu.make_async_copy(wide.at[m, n], window, sems.at[m, n])
            copy.start()
            copies.append(copy)
    for copy in copies:
        copy.wait()


def write_taps(device, parts, shifts, groups, targets, shape, buffer, name, returned=None, after=()):
    extra, place = [] if buffer is None else [buffer], returned or []
    outs, aliases = [shape_of(shape, F32)], {}
    if place:
        outs.append(shape_of(place[1].shape, place[1].dtype))
        aliases[2 + len(parts)] = 1
    if extra:
        aliases[1 + len(parts) + len(place)] = 0
    results = call(
        functools.partial(write_taps_body, shifts, groups, targets, len(extra), len(place) // 2), device,
        (*parts, *place, *extra), [WHOLE] * len(parts) + [HBM] * (len(place) + len(extra)), outs, [HBM] * len(outs),
        scratch=[
            pltpu.VMEM((len(parts), *parts[0].shape), F32), pltpu.SemaphoreType.DMA((len(parts), len(targets))),
            *[pltpu.SemaphoreType.DMA] * (len(place) // 2),
        ],
        aliases=aliases, name=name, after=after,
    )
    return results


def act_body(meta, x, *acts):
    act = gelu(x[...].astype(F32)).astype(BF16)
    cols = acts[0].shape[1]
    for n, ref in enumerate(acts):
        ref[...] = act[:, n * cols : (n + 1) * cols]


def mm_parts(lefts, weight):
    cols = lefts[0].shape[1]
    return sum(mm(left[...], weight[0, n * cols : (n + 1) * cols]) for n, left in enumerate(lefts))


def mm_back_parts(lefts, weight):
    cols = lefts[0].shape[1]
    return sum(mm_back(left[...], weight[0, :, n * cols : (n + 1) * cols]) for n, left in enumerate(lefts))


def oth_out_body(meta, x0, x1, oth0, oth1, far0, far1, own0, own1, w_near, w_mid, w_far, out):
    cols = x0.shape[1]
    conv = mm_parts((oth0, oth1), w_mid) + mm_parts((far0, far1), w_near) + mm_parts((own0, own1), w_far)
    out[:, :cols] = (x0[...].astype(F32) + conv[:, :cols]).astype(BF16)
    out[:, cols:] = (x1[...].astype(F32) + conv[:, cols:]).astype(BF16)


def own_out_body(meta, x, own0, own1, oth0, oth1, far0, far1, w_near, w_mid, w_far, out):
    conv = mm_parts((own0, own1), w_mid) + mm_parts((oth0, oth1), w_near) + mm_parts((far0, far1), w_far)
    out[...] = (x[...].astype(F32) + conv).astype(BF16)


def outer_first_body(steps, count, meta, own0, own1, oth0, oth1, far0, far1, own_far0, own_far1, u_own, u_oth, mid, *refs):
    keep, send, rest, total = refs
    i = pl.program_id(0)

    @pl.when(i == 0)
    def _():
        total[...] = jnp.zeros_like(total)
        rest[...] = jnp.zeros_like(rest)

    cols = own0.shape[1]
    for n, (own, oth, far, own_far) in enumerate(((own0, oth0, far0, own_far0), (own1, oth1, far1, own_far1))):
        rows = slice(n * cols, (n + 1) * cols)
        u_first, u_second = u_own[:, :cols], u_own[:, cols:]
        total[0, rows] += mm_outer(own[...], u_oth[...]) + mm_outer(own_far[...], u_first)
        total[1, rows] += mm_outer(far[...], u_oth[...]) + mm_outer(oth[...], u_first)
        rest[0, rows] += mm_outer(own_far[...], u_second)
        rest[1, rows] += mm_outer(oth[...], u_second)

    @pl.when(i == steps - 1)
    def _():
        lead = 0
        for part in (mid, total):
            window = pl.ds(lead, part.shape[0])
            split_into(part, meta[CORE], count, keep.at[window], [send.at[window]])
            lead += part.shape[0]


def outer_second_body(steps, count, meta, own0, own1, far0, far1, u_oth, rest, keep, send, total):
    i = pl.program_id(0)

    @pl.when(i == 0)
    def _():
        total[...] = rest[...]

    cols = own0.shape[1]
    for n, (own, far) in enumerate(((own0, far0), (own1, far1))):
        rows = slice(n * cols, (n + 1) * cols)
        total[0, rows] += mm_outer(own[...], u_oth[...])
        total[1, rows] += mm_outer(far[...], u_oth[...])

    @pl.when(i == steps - 1)
    def _():
        split_into(total, meta[CORE], count, keep, [send])


def oth_grad_body(meta, x0, x1, u_own, oth0, oth1, far, w_near, w_mid, w_far, grad):
    cols = oth0.shape[1]
    grad_act = mm_back(u_own[...], w_near[0]) + mm_back_parts((oth0, oth1), w_mid) + mm_back(far[...], w_far[0])
    for n, (x, u) in enumerate(((x0, oth0), (x1, oth1))):
        part = slice(n * cols, (n + 1) * cols)
        _, slope = gelu_and_slope(x[...].astype(F32))
        grad[:, part] = (u[...].astype(F32) + slope * grad_act[:, part]).astype(BF16)


def own_grad_body(
    steps, meta, x, u_own, oth0, oth1, far0, far1, w_near, w_mid, w_far, returned, buffer, grad, out, sem
):
    i = pl.program_id(0)
    copy = returned_copy(meta, returned, out, sem)

    @pl.when(i == 0)
    def _():
        copy.start()

    _, slope = gelu_and_slope(x[...].astype(F32))
    u = u_own[...]
    grad_act = mm_back(u, w_mid[0]) + mm_back_parts((oth0, oth1), w_far) + mm_back_parts((far0, far1), w_near)
    grad[...] = (u.astype(F32) + slope * grad_act).astype(BF16)

    @pl.when(i == steps - 1)
    def _():
        copy.wait()


def per_device(genome, conv_weight, upstream):
    genome, upstream = genome[0], upstream[0]
    bins, chans = genome.shape
    half, cols = bins // 2, chans // 2
    block = half // 4
    steps = half // block
    count = lax.axis_size("seq")
    index = lax.axis_index("seq")
    tap = DILATION_BINS // bins
    span = 2 * tap
    dp_count, along_count = lax.axis_size("dp"), count // span
    side, along = lax.rem(index // tap, 2), index // span
    if along_count % 2 == 0:
        along = along ^ side
    def is_even(i):
        return (i // tap) % 2 == 0

    swap_pairs = [(i, i + tap if is_even(i) else i - tap) for i in range(count)]
    outer_pairs = [(i, i - span if is_even(i) else i + span) for i in range(count)]
    outer_pairs = [(i, j) for i, j in outer_pairs if 0 <= j < count]
    inner_pairs = [(j, i) for i, j in outer_pairs]

    def swap(value):
        return lax.ppermute(value, "seq", swap_pairs)

    def outward(value):
        return lax.ppermute(value, "seq", outer_pairs)

    def inward(value):
        return lax.ppermute(value, "seq", inner_pairs)

    def to_core(value, shift=1):
        return lax.ppermute(value, "seq", [(i, i - i % tap + (i % tap + shift) % tap) for i in range(count)])

    def to_dp(value, shift=1):
        return lax.ppermute(value, "dp", [(i, (i + shift) % dp_count) for i in range(dp_count)])

    flip = 1 if along_count % 2 == 0 else 0
    bits = (along_count - 1).bit_length()
    halving = along_count == 1 << bits

    def reversed_bits(value):
        return sum(((value >> n) & 1) << (bits - 1 - n) for n in range(bits)) if halving else value

    def place_along(i):
        return reversed_bits((i // span) ^ (flip * ((i // tap) % 2)))

    def device_at(i, side, position):
        return (reversed_bits(position) ^ (flip * side)) * span + side * tap + i % tap

    def to_along(value, move):
        pairs = [(i, device_at(i, (i // tap) % 2, move(place_along(i)))) for i in range(count)]
        return lax.ppermute(value, "seq", pairs)

    def to_side(value):
        pairs = [(i, device_at(i, 1 - (i // tap) % 2, place_along(i))) for i in range(count)]
        return lax.ppermute(value, "seq", pairs)

    rows_spec = pl.BlockSpec((block, chans), lambda i, s: (i, 0))
    own_spec = pl.BlockSpec((block, chans), lambda i, s: (s[SIDE] * steps + i, 0))
    w_near = pl.BlockSpec((1, chans, chans), lambda i, s: (2 - 2 * s[SIDE], 0, 0))
    w_mid = pl.BlockSpec((1, chans, chans), lambda i, s: (1, 0, 0))
    w_far = pl.BlockSpec((1, chans, chans), lambda i, s: (2 * s[SIDE], 0, 0))
    half_shape, whole_shape = shape_of((half, chans), BF16), shape_of((bins, chans), BF16)
    along = reversed_bits(along)
    along_bits = [(along >> n) & 1 for n in reversed(range(bits))]
    meta = jnp.stack([side, lax.rem(index, tap), lax.axis_index("dp"), along, *along_bits]).astype(jnp.int32)
    device = Device(meta)

    part_spec = pl.BlockSpec((block, cols), lambda i, s: (i, 0))
    part_wide = pl.BlockSpec((2 * block, cols), lambda i, s: (i, 0))
    rows_wide = pl.BlockSpec((2 * block, chans), lambda i, s: (i, 0))
    own_wide = pl.BlockSpec((2 * block, chans), lambda i, s: (s[SIDE] * (steps // 2) + i, 0))
    weights, weight_specs = (conv_weight,) * 3, [w_near, w_mid, w_far]

    staged = halving and (chans // tap // dp_count) % (16 * along_count) == 0

    def core_stage(parts, name, after=()):
        keep, send = parts
        keep, send = reduce(device, [[keep, to_core(send)]], dp_count, DP, dtype=BF16, name=name + "_core", after=after)
        return [keep, to_dp(send)]

    def along_stage(groups, step, after=()):
        if not staged:
            return reduce(device, groups, name=f"along{step}", after=after)
        keep, send = reduce(device, groups, 2, ALONG_BITS + step, dtype=BF16, name=f"along{step}", after=after)
        return [keep, to_along(send, lambda position: position ^ (1 << (bits - 1 - step)))]

    def side_stage(groups, after=()):
        (total,) = reduce(device, groups, swap_from=2, name="last", after=after)
        if not staged:
            together = [[i + span * j for j in range(along_count)] for i in range(span)]
            total = lax.psum(total, "seq", axis_index_groups=together)
        return [total, to_side(total)]

    def round_slice(parts, after=()):
        return reduce(device, [parts], dtype=BF16, name="side", after=after)[0]

    def spread(value):
        moves = [lambda position, s=s: (position + s) % along_count for s in range(1, along_count)]
        return [value] + [to_along(value, move) for move in moves if staged]

    def join(pieces, name, after=()):
        total = gather(device, pieces, ALONG, name, after) if staged else pieces[0]
        return [total] + [to_core(total, s) for s in range(1, tap)]

    targets = [(1, 0), (1, cols), (0, 0), (2, 0), (0, cols), (2, cols)]

    def write(joined, dp_shift, buffer, returned=None, after=()):
        shifts = [(core_shift, dp_shift) for core_shift in range(tap)]
        return write_taps(
            device, joined, shifts, (tap, dp_count), targets, conv_weight.shape, buffer, f"write_taps{dp_shift}",
            returned, after,
        )

    def slices_of(parts, dtype):
        piece = (parts, chans // tap, cols)
        return [shape_of(piece, F32), shape_of(piece, dtype)], [pl.BlockSpec(piece, lambda i, s: (0, 0, 0))] * 2

    sums_shape = (2, chans, cols)
    sums_spec = pl.BlockSpec(sums_shape, lambda i, s: (0, 0, 0))

    def oth_act(x, name, after=()):
        return call(
            act_body, device, (x,), [part_spec], shape_of((half, cols), BF16), part_spec, grid=(steps,), name=name,
            after=after,
        )

    (x_send0,) = cut(device, (genome,), [(0, False, 0, half, cols)], "cut_first")
    x_oth0 = swap(x_send0)
    a_own = call(
        act_body, device, (genome,), [own_spec], [shape_of((half, cols), BF16)] * 2, [part_spec] * 2, grid=(steps,),
        name="own_act",
    )
    a_oth_far = [outward(part) for part in a_own]
    x_send1, u_send0, u_send1, u_own = cut(
        device, (genome, upstream),
        [(0, False, cols, half, cols), (1, False, 0, half, cols), (1, False, cols, half, cols), (1, True, 0, half, chans)],
        "cut_rest",
    )
    x_oth1, u_oth = swap(x_send1), [swap(u_send0), swap(u_send1)]
    u_oth_far, u_own_far = outward(u_own), [inward(part) for part in u_oth]
    mid = call(
        lambda meta, *refs: mid_body(*refs), device, (genome, upstream), [rows_spec] * 2, shape_of(sums_shape, F32),
        sums_spec, grid=(2 * steps,), name="mid_tap",
    )
    a_oth0 = oth_act(x_oth0, "oth_act0")
    a_own_far0 = inward(a_oth0)
    a_oth1 = oth_act(x_oth1, "oth_act1")
    a_own_far1 = inward(a_oth1)
    out = call(
        oth_out_body, device, (x_oth0, x_oth1, a_oth0, a_oth1, *a_oth_far, *a_own, *weights),
        [*[part_spec] * 8, *weight_specs], half_shape, rows_spec, grid=(steps,), name="oth_out", after=(a_own_far0,),
    )
    out = swap(out)
    slices, specs = slices_of(4, BF16)
    *outer0, rest = call(
        functools.partial(outer_first_body, steps, tap), device,
        (*a_own, a_oth0, a_oth1, *a_oth_far, a_own_far0, a_own_far1, u_own, u_oth[0], mid),
        [*[part_spec] * 8, rows_spec, part_spec, WHOLE], [*slices, shape_of(sums_shape, F32)], [*specs, sums_spec],
        grid=(steps,), scratch=[pltpu.VMEM(sums_shape, F32)], name="outer_first",
    )
    slices, specs = slices_of(2, F32)
    outer1 = call(
        functools.partial(outer_second_body, steps, tap), device, (*a_own, *a_oth_far, u_oth[1], rest),
        [*[part_spec] * 5, WHOLE], slices, specs, grid=(steps,), scratch=[pltpu.VMEM(sums_shape, F32)],
        name="outer_second",
    )
    outer0 = core_stage(outer0, "outer0", after=(u_own_far[0],))
    outer1 = core_stage(outer1, "outer1")
    grad = call(
        oth_grad_body, device, (x_oth0, x_oth1, u_own, *u_oth, u_oth_far, *weights),
        [part_spec, part_spec, rows_spec, part_spec, part_spec, rows_spec, *weight_specs], half_shape, rows_spec,
        grid=(steps,), name="oth_grad",
    )
    grad = swap(grad)
    parts = along_stage([outer0, outer1], 0)
    output = call(
        own_out_body, device, (genome, *a_own, a_oth0, a_oth1, a_own_far0, a_own_far1, *weights),
        [own_spec, *[part_spec] * 6, *weight_specs], whole_shape, own_spec, grid=(steps,), name="own_out",
    )
    parts = along_stage([parts], 1)
    grad_genome, output = call(
        functools.partial(own_grad_body, steps // 2), device,
        (genome, u_own, *u_oth, *u_own_far, *weights, out, output),
        [own_wide, rows_wide, *[part_wide] * 4, *weight_specs, HBM, HBM], [whole_shape] * 2, [own_wide, HBM],
        grid=(steps // 2,), scratch=[pltpu.SemaphoreType.DMA], aliases={11: 1}, name="own_grad",
    )
    parts = side_stage([parts])
    last_slice = round_slice(parts)
    far_slices = [to_dp(last_slice, s) for s in range(1, dp_count)]
    pieces = spread(last_slice)
    far_pieces = [[far] + [to_dp(piece, s) for piece in pieces[1:]] for s, far in enumerate(far_slices, 1)]
    joined = join(pieces, "join")
    joined_far = [join(far, f"join_far{s}") for s, far in enumerate(far_pieces, 1)]
    grad_weight, grad_genome = write(joined, 0, None, [grad, grad_genome])
    for s, far in enumerate(joined_far, 1):
        (grad_weight,) = write(far, s, grad_weight)
    return (output[None], grad_genome[None], grad_weight)


def solution(mesh):
    return jax.shard_map(
        per_device,
        mesh=mesh,
        in_specs=(P("dp", "seq", None), P(), P("dp", "seq", None)),
        out_specs=(P("dp", "seq", None), P("dp", "seq", None), P()),
        check_vma=False,
    )
```
